256 devices in a mesh: dp: 8 (over z), cand: 32 (over y, x, core).
Axes of the slice: x: 4, y: 4, z: 8, core: 2. Of those that a mesh axis runs over, the one named last changes fastest.
Arguments:
- queries: bfloat16 [128, 32, 32, 128], P('dp', 'cand'), may hold values from -1 to 1, as said below
- passages: bfloat16 [128, 8, 256, 128], P('cand'), may hold values from -1 to 1, as said below
- cand_ids: int32 [128, 2], P('dp'), may hold values from 0 to 127, as said below
- pos_index: int32 [128, 32], P('dp'), may hold values from 0 to 15
Outputs:
- losses: float32 [128, 32], P('dp', 'cand')
- query_grads: float32 [128, 32, 32, 128], P('dp', 'cand')
- passage_grads: float32 [128, 8, 256, 128], P('cand', 'dp')
The draws below stay inside these ranges and needn't reach their ends.
Inputs may be any that keep to these rules, and one draw needn't show every extreme that they name: `queries`: every token vector has unit length. `passages`: every token vector has unit length. `cand_ids`: block k is stored on index k // 4 of cand. Within the 16 rows of one index of dp, at most 4 of the entries name blocks stored on one index of cand, and in every such group of rows some index of cand is named by exactly 4 entries. The two entries of a row may be equal.
All inputs are finite; a program needn't handle non-finite values.
Results may differ from the reference program's by a relative error of at most 0.0003.
Values may be sent and summed in bfloat16 or wider, within the bound.
A program may use at most 128 MiB of HBM per device.

```python
import jax
import jax.numpy as jnp
from jax import lax

D = 128
LQ = 32
LP = 256
QPB = 32
PPB = 8
PB_DEV = 4
QB = 16
NQB = 128
NPB = 128
CAP = 4


def to_unit(entries):
    return entries / jnp.sqrt(jnp.sum(entries * entries, -1, keepdims=True))


def draw_queries(key, part):
    key = jax.random.fold_in(key, 5)
    entries = jax.random.normal(key, (NQB, QPB, LQ, D), jnp.float32)
    return to_unit(entries).astype(jnp.bfloat16)


def draw_passages(key, part):
    key = jax.random.fold_in(key, 7)
    entries = jax.random.normal(key, (NPB, PPB, LP, D), jnp.float32)
    return to_unit(entries).astype(jnp.bfloat16)


def draw_cand_ids(key, part):
    key = jax.random.fold_in(key, 11)
    owner_total = NPB // PB_DEV
    row_groups = NQB // QB
    requests = 2 * QB

    def one_group(group_key):
        subkeys = jax.random.split(group_key, 4)
        hot_owner = jax.random.randint(subkeys[0], (), 0, owner_total)
        copies = jnp.arange(owner_total * CAP, dtype=jnp.int32)
        owner_of = copies // CAP
        rank_values = jax.random.permutation(subkeys[1], owner_total * CAP).astype(jnp.int32)
        rank_values = jnp.where(owner_of == hot_owner, copies - owner_total * CAP, rank_values)
        ordering = jnp.argsort(rank_values, stable=True)
        chosen = owner_of[ordering[:requests]]
        chosen = chosen[jax.random.permutation(subkeys[2], requests)]
        local_ids = jax.random.randint(subkeys[3], (requests,), 0, PB_DEV)
        return (chosen * PB_DEV + local_ids).reshape(QB, 2)
    group_keys = jax.random.split(key, row_groups)
    return jax.vmap(one_group)(group_keys).reshape(NQB, 2).astype(jnp.int32)


def place_ends(drawn, rng, least, top_value):
    dims = drawn.shape
    place = [jax.random.randint(jax.random.fold_in(rng, axis), (), 0, dims[axis]) for axis in range(len(dims))]
    drawn = drawn.at[tuple(place)].set(least)
    longest = dims.index(max(dims))
    place[longest] = (place[longest] + 1) % dims[longest]
    return drawn.at[tuple(place)].set(top_value)


def setup_inputs(seed: int = 0) -> dict:
    keys = jax.random.split(jax.random.key(seed), 5)
    queries = draw_queries(jax.random.fold_in(keys[4], 71), 0)
    passages = draw_passages(jax.random.fold_in(keys[4], 71), 0)
    cand_ids = draw_cand_ids(jax.random.fold_in(keys[4], 71), 0)
    pos_index = place_ends(jax.random.randint(keys[3], (NQB, QPB), 0, 2 * PPB), jax.random.fold_in(keys[3], 1), 0, (2 * PPB) - 1).astype(jnp.int32)
    return {"queries": queries, "passages": passages, "cand_ids": cand_ids, "pos_index": pos_index}


softness = 0.05
loss_scale = 32.0


def slot_tiles(query_block, passage_block):
    query_flat = query_block.reshape(-1, query_block.shape[-1])
    passage_flat = passage_block.reshape(-1, passage_block.shape[-1])
    similar = lax.dot_general(query_flat, passage_flat, (((1,), (1,)), ((), ())), preferred_element_type=jnp.float32)
    exponent = jnp.exp(similar / softness).reshape(query_flat.shape[0], passage_block.shape[0], passage_block.shape[1])
    totals = jnp.sum(exponent, -1)
    weights = exponent / totals[:, :, None]
    soft_max = softness * jnp.log(totals)
    scores = jnp.sum(soft_max.reshape(query_block.shape[0], query_block.shape[1], passage_block.shape[0]), 1)
    return scores, weights, query_flat, passage_flat


def tile_grads(weights, grad_tile, query_flat, passage_flat, tokens):
    expanded = jnp.repeat(grad_tile, tokens, axis=0)
    sim_grad = (weights * expanded[:, :, None]).reshape(query_flat.shape[0], passage_flat.shape[0])
    query_wide = query_flat.astype(jnp.float32)
    passage_wide = passage_flat.astype(jnp.float32)
    query_grad = jnp.dot(sim_grad, passage_wide, precision=lax.Precision.HIGHEST, preferred_element_type=jnp.float32)
    passage_grad = lax.dot_general(sim_grad, query_wide, (((0,), (0,)), ((), ())), precision=lax.Precision.HIGHEST, preferred_element_type=jnp.float32)
    return query_grad, passage_grad


def reference(queries, passages, cand_ids, pos_index):
    per_block = passages.shape[1]
    tokens = queries.shape[2]

    def one_block(passage_acc, inputs):
        query_block, pair_ids, positive = inputs
        first_scores, first_weights, query_flat, first_flat = slot_tiles(query_block, passages[pair_ids[0]])
        second_scores, second_weights, query_again, second_flat = slot_tiles(query_block, passages[pair_ids[1]])
        logits = jnp.concatenate([first_scores, second_scores], 1)
        log_total = jnp.log(jnp.sum(jnp.exp(logits), -1))
        onehot = (jnp.arange(2 * per_block, dtype=jnp.int32)[None, :] == positive[:, None]).astype(jnp.float32)
        row_losses = log_total - jnp.sum(logits * onehot, -1)
        dlogit = loss_scale * (jnp.exp(logits - log_total[:, None]) - onehot)
        first_query, first_passage = tile_grads(first_weights, dlogit[:, :per_block], query_flat, first_flat, tokens)
        second_query, second_passage = tile_grads(second_weights, dlogit[:, per_block:], query_flat, second_flat, tokens)
        passage_acc = passage_acc.at[pair_ids[0]].add(first_passage.reshape(passages.shape[1:]))
        passage_acc = passage_acc.at[pair_ids[1]].add(second_passage.reshape(passages.shape[1:]))
        return passage_acc, (row_losses, (first_query + second_query).reshape(query_block.shape))

    initial = jnp.zeros(passages.shape, jnp.float32)
    passage_acc, outputs = lax.scan(one_block, initial, (queries, cand_ids, pos_index))
    return outputs[0], outputs[1], passage_acc
```

```python
import functools
import math

import jax
import jax.numpy as jnp
from jax import lax
from jax.experimental import pallas as pl
from jax.experimental.pallas import tpu as pltpu
from jax.sharding import PartitionSpec as P

softness = 0.05
loss_scale = 32.0
to_exp2 = math.log2(math.e) / softness
MESH = pl.DeviceIdType.MESH
HIGHEST = lax.Precision.HIGHEST
LANES = 128


def tables_kernel(blocks_here, cap, ids_ref, request_ref, place_ref, counts_ref):
    def clear_count(owner, _):
        counts_ref[owner] = 0
        return 0

    def clear_request(place, _):
        request_ref[place] = -1
        return 0

    def put(request, _):
        owner = ids_ref[request] // blocks_here
        slot = counts_ref[owner]
        counts_ref[owner] = slot + 1
        request_ref[owner * cap + slot] = request
        place_ref[request] = owner * cap + slot
        return 0

    lax.fori_loop(0, counts_ref.shape[0], clear_count, 0)
    lax.fori_loop(0, request_ref.shape[0], clear_request, 0)
    lax.fori_loop(0, ids_ref.shape[0], put, 0)


def main_kernel(
    rows,
    ring,
    cap,
    request_ref,
    place_ref,
    ids_ref,
    q_ref,
    p_ref,
    pos_ref,
    loss_ref,
    query_out,
    passage_out,
    q_send,
    q_slot,
    e_buf,
    totals,
    scores,
    grad_t,
    grad_slot,
    grad_back,
    acc,
    z_buf,
    send_sem,
    q_sem,
    score_sem,
    back_sem,
    z_send_sem,
    z_recv_sem,
):
    row_blocks, tokens, width = q_ref.shape
    blocks_here, per_block, passage_len, _ = p_ref.shape
    flat = rows * tokens
    me = lax.axis_index("cand")
    plane = lax.axis_index("dp")
    half_blocks = blocks_here // 2

    def peer_of(offset):
        return lax.rem(me + offset, rows)

    barrier = pltpu.get_barrier_semaphore()

    def greet(offset, _):
        pl.semaphore_signal(
            barrier, inc=1, device_id={"cand": peer_of(offset)}, device_id_type=MESH
        )
        return 0

    lax.fori_loop(1, rows, greet, 0)
    up, down = lax.rem(plane + 1, ring), lax.rem(plane + ring - 1, ring)
    for neighbour in (up, down):
        pl.semaphore_signal(barrier, inc=1, device_id={"dp": neighbour}, device_id_type=MESH)

    def fill(owner, _):
        for slot in range(cap):
            request = jnp.maximum(request_ref[owner * cap + slot], 0)
            q_send[slot, owner] = q_ref[request // 2]
        return 0

    lax.fori_loop(0, rows, fill, 0)
    my_rows = pl.ds(pl.multiple_of(me * tokens, tokens), tokens)
    pl.semaphore_wait(barrier, rows - 1 + 2)

    def q_copy(slot, peer):
        return pltpu.make_async_remote_copy(
            src_ref=q_send.at[slot, peer],
            dst_ref=q_slot.at[slot, my_rows],
            send_sem=send_sem.at[0],
            recv_sem=q_sem.at[slot],
            device_id={"cand": peer},
            device_id_type=MESH,
        )

    for slot in range(cap):

        def send_queries(offset, _, slot=slot):
            q_copy(slot, peer_of(offset)).start()
            return 0

        lax.fori_loop(1, rows, send_queries, 0)
        q_slot[slot, my_rows] = q_send[slot, me]

    head = pl.ds(0, flat - tokens)
    lane = lax.broadcasted_iota(jnp.int32, (flat, LANES), 1)
    query_of = lax.broadcasted_iota(jnp.int32, (flat, LANES), 0) // tokens
    my_scores = jnp.zeros((per_block, LANES), jnp.float32)

    def my_request(slot):
        return request_ref[me * cap + slot]

    def my_block(slot):
        return ids_ref[jnp.maximum(my_request(slot), 0)] % blocks_here

    def forward(slot, my_scores):
        pltpu.make_async_copy(q_slot.at[slot, head], q_slot.at[slot, head], q_sem.at[slot]).wait()
        block = my_block(slot)

        def candidate(c, _):
            similar = lax.dot_general(
                p_ref[block, c],
                q_slot[slot],
                (((1,), (1,)), ((), ())),
                preferred_element_type=jnp.float32,
            )
            exponent = jnp.exp2(similar * to_exp2)
            e_buf[slot, c] = exponent
            totals[slot, pl.ds(c, 1)] = jnp.sum(exponent, 0, keepdims=True)
            return 0

        lax.fori_loop(0, per_block, candidate, 0)
        soft_max = softness * jnp.log(totals[slot])
        place = (query_of + slot * rows == lane).astype(jnp.float32)
        return my_scores + jnp.dot(
            soft_max, place, precision=HIGHEST, preferred_element_type=jnp.float32
        )

    my_scores = lax.fori_loop(0, cap, forward, my_scores)
    scores[me] = my_scores

    def score_copy(peer):
        return pltpu.make_async_remote_copy(
            src_ref=scores.at[me],
            dst_ref=scores.at[me],
            send_sem=send_sem.at[1],
            recv_sem=score_sem,
            device_id={"cand": peer},
            device_id_type=MESH,
        )

    def send_scores(offset, _):
        score_copy(peer_of(offset)).start()
        return 0

    lax.fori_loop(1, rows, send_scores, 0)
    others = pl.ds(0, rows - 1)
    pltpu.make_async_copy(scores.at[others], scores.at[others], score_sem).wait()

    lane_in = lax.broadcasted_iota(jnp.int32, (LANES, rows), 0)
    query_in = lax.broadcasted_iota(jnp.int32, (LANES, rows), 1)

    def scores_of(place):
        pick = (lane_in == query_in + (place % cap) * rows).astype(jnp.float32)
        return jnp.dot(
            scores[place // cap], pick, precision=HIGHEST, preferred_element_type=jnp.float32
        )

    column = lax.broadcasted_iota(jnp.int32, (per_block, rows), 0)
    spread = (
        lax.broadcasted_iota(jnp.int32, (rows, flat), 1) // tokens
        == lax.broadcasted_iota(jnp.int32, (rows, flat), 0)
    ).astype(jnp.float32)

    def factors(slot, _):
        request = my_request(slot)
        valid = jnp.where(request >= 0, loss_scale, 0.0)
        request = jnp.maximum(request, 0)
        block_row, half = request // 2, request % 2
        mine = scores_of(me * cap + slot)
        other = scores_of(place_ref[block_row * 2 + 1 - half])
        log_total = jnp.log(
            jnp.sum(jnp.exp(mine), 0, keepdims=True) + jnp.sum(jnp.exp(other), 0, keepdims=True)
        )
        onehot = (column + half * per_block == pos_ref[block_row]).astype(jnp.float32)
        dlogit = valid * (jnp.exp(mine - log_total) - onehot)
        wide = jnp.dot(dlogit, spread, precision=HIGHEST, preferred_element_type=jnp.float32)
        totals[slot] = wide / totals[slot]
        return 0

    lax.fori_loop(0, cap, factors, 0)

    plus, minus = ring // 2, ring - 1 - ring // 2
    chains = []
    first = 0
    for half, sign, length in ((0, 1, plus), (0, -1, minus), (1, 1, minus), (1, -1, plus)):
        chains.append((half, sign, length, first))
        first += length

    def plane_at(offset):
        return lax.rem(plane + offset + ring, ring)

    def z_copy(chain, step):
        half, sign, length, first = chain
        if step == 0:
            source = acc.at[plane_at(sign * length), pl.ds(half * half_blocks, half_blocks)]
        else:
            source = z_buf.at[first + step - 1]
        return pltpu.make_async_remote_copy(
            src_ref=source,
            dst_ref=z_buf.at[first + step],
            send_sem=z_send_sem.at[first + step],
            recv_sem=z_recv_sem.at[first + step],
            device_id={"dp": up if sign > 0 else down},
            device_id_type=MESH,
        )

    grad_t[...] = jnp.zeros_like(grad_t)

    def gradients(step, _):
        near = jnp.where(step % 2 == 1, ring // 2 - (step + 1) // 2, step // 2 + ring // 2)
        c = lax.rem(plane + near, ring)
        acc[c] = jnp.zeros(acc.shape[1:], jnp.float32)

        def one_slot(slot, _):
            block = my_block(slot)
            passage = p_ref[block, c]
            queries = q_slot[slot]
            sim_grad = e_buf[slot, c] * totals[slot, pl.ds(c, 1)]
            high = sim_grad.astype(jnp.bfloat16)
            low = (sim_grad - high.astype(jnp.float32)).astype(jnp.bfloat16)
            passage_grad = jnp.dot(high, queries, preferred_element_type=jnp.float32) + jnp.dot(
                low, queries, preferred_element_type=jnp.float32
            )
            for local in range(blocks_here):
                chosen = jnp.where(block == local, 1.0, 0.0)
                acc[c, local] += chosen * passage_grad
            across = (((0,), (0,)), ((), ()))
            grad_t[slot] += lax.dot_general(
                passage, high, across, preferred_element_type=jnp.float32
            ) + lax.dot_general(passage, low, across, preferred_element_type=jnp.float32)
            return 0

        lax.fori_loop(0, cap, one_slot, 0)
        for chain in chains:
            half, sign, length, first = chain
            if length:
                at = [k for k in range(ring) if order[k] % ring == (sign * length) % ring][0]

                @pl.when(step == at)
                def _(chain=chain):
                    z_copy(chain, 0).start()

        return 0

    order = [
        ring // 2 - (k + 1) // 2 if k % 2 == 1 else k // 2 + ring // 2 for k in range(ring)
    ]
    lax.fori_loop(0, per_block, gradients, 0)

    def back_copy(peer):
        peer_rows = pl.ds(pl.multiple_of(peer * tokens, tokens), tokens)
        return pltpu.make_async_remote_copy(
            src_ref=grad_slot.at[:, peer_rows],
            dst_ref=grad_back.at[me],
            send_sem=send_sem.at[2],
            recv_sem=back_sem,
            device_id={"cand": peer},
            device_id_type=MESH,
        )

    def turn(slot, _):
        grad_slot[slot] = grad_t[slot].T
        return 0

    lax.fori_loop(0, cap, turn, 0)

    def send_back(offset, _):
        back_copy(peer_of(offset)).start()
        return 0

    lax.fori_loop(1, rows, send_back, 0)
    grad_back[me] = grad_slot[:, my_rows]

    for step in range(1, plus):
        for chain in chains:
            half, sign, length, first = chain
            if step < length:
                z_copy(chain, step - 1).wait_recv()
                target = plane_at(sign * (length - step))
                z_buf[first + step - 1] += acc[target, pl.ds(half * half_blocks, half_blocks)]
                z_copy(chain, step).start()

    def loss_row(block_row, _):
        first = scores_of(place_ref[2 * block_row])
        second = scores_of(place_ref[2 * block_row + 1])
        log_total = jnp.log(
            jnp.sum(jnp.exp(first), 0, keepdims=True) + jnp.sum(jnp.exp(second), 0, keepdims=True)
        )
        positive = pos_ref[block_row]
        chosen = jnp.sum(jnp.where(column == positive, first, 0.0), 0, keepdims=True) + jnp.sum(
            jnp.where(column + per_block == positive, second, 0.0), 0, keepdims=True
        )
        here = lax.broadcasted_iota(jnp.int32, (1, rows), 1) == me
        loss = jnp.sum(jnp.where(here, log_total - chosen, 0.0), 1, keepdims=True)
        loss_ref[pl.ds(block_row, 1)] = loss
        return 0

    lax.fori_loop(0, row_blocks, loss_row, 0)

    pltpu.make_async_copy(grad_back.at[others], grad_back.at[others], back_sem).wait()

    def add_pair(block_row, _):
        one, two = place_ref[2 * block_row], place_ref[2 * block_row + 1]
        query_out[block_row] = grad_back[one // cap, one % cap] + grad_back[two // cap, two % cap]
        return 0

    lax.fori_loop(0, row_blocks, add_pair, 0)

    for half in range(2):
        here = pl.ds(half * half_blocks, half_blocks)
        result = acc[plane, here]
        for chain in chains:
            if chain[0] == half and chain[2]:
                z_copy(chain, chain[2] - 1).wait_recv()
                result = result + z_buf[chain[3] + chain[2] - 1]
        passage_out[here] = result

    for slot in range(cap):
        pltpu.make_async_copy(q_slot.at[slot, head], q_slot.at[slot, head], send_sem.at[0]).wait()
    pltpu.make_async_copy(scores.at[others], scores.at[others], send_sem.at[1]).wait()
    pltpu.make_async_copy(grad_back.at[others], grad_back.at[others], send_sem.at[2]).wait()
    for chain in chains:
        for step in range(chain[2]):
            z_copy(chain, step).wait_send()


def on_device(rows, ring, queries, passages, cand_ids, pos_index):
    row_blocks, _, tokens, width = queries.shape
    blocks_here, per_block, passage_len, _ = passages.shape
    requests = 2 * row_blocks
    cap = 4 * ((requests + rows - 1) // rows)
    flat = rows * tokens
    smem = pl.BlockSpec(memory_space=pltpu.SMEM)
    vmem = pl.BlockSpec(memory_space=pltpu.VMEM)
    flat_ids = cand_ids.reshape(-1)
    request_at, place_of = pl.pallas_call(
        functools.partial(tables_kernel, blocks_here, cap),
        out_shape=(
            jax.ShapeDtypeStruct((rows * cap,), jnp.int32),
            jax.ShapeDtypeStruct((requests,), jnp.int32),
        ),
        in_specs=[smem],
        out_specs=(smem, smem),
        scratch_shapes=[pltpu.SMEM((rows,), jnp.int32)],
        name="tables",
    )(flat_ids)
    half_blocks = blocks_here // 2
    hops = 2 * (ring - 1)
    f32, bf16 = jnp.float32, jnp.bfloat16
    losses, query_grads, passage_grads = pl.pallas_call(
        functools.partial(main_kernel, rows, ring, cap),
        out_shape=(
            jax.ShapeDtypeStruct((row_blocks, 1), f32),
            jax.ShapeDtypeStruct((row_blocks, tokens, width), f32),
            jax.ShapeDtypeStruct((blocks_here, passage_len, width), f32),
        ),
        in_specs=[smem] * 3 + [vmem] * 3,
        out_specs=(vmem, vmem, vmem),
        scratch_shapes=[
            pltpu.VMEM((cap, rows, tokens, width), bf16),
            pltpu.VMEM((cap, flat, width), bf16),
            pltpu.VMEM((cap, per_block, passage_len, flat), f32),
            pltpu.VMEM((cap, per_block, flat), f32),
            pltpu.VMEM((rows, per_block, LANES), f32),
            pltpu.VMEM((cap, width, flat), f32),
            pltpu.VMEM((cap, flat, width), f32),
            pltpu.VMEM((rows, cap, tokens, width), f32),
            pltpu.VMEM((per_block, blocks_here, passage_len, width), f32),
            pltpu.VMEM((hops, half_blocks, passage_len, width), f32),
            pltpu.SemaphoreType.DMA((3,)),
            pltpu.SemaphoreType.DMA((cap,)),
            pltpu.SemaphoreType.DMA,
            pltpu.SemaphoreType.DMA,
            pltpu.SemaphoreType.DMA((hops,)),
            pltpu.SemaphoreType.DMA((hops,)),
        ],
        compiler_params=pltpu.CompilerParams(
            collective_id=0, has_side_effects=True, vmem_limit_bytes=60 * 1024 * 1024
        ),
        name="late_interaction",
    )(
        request_at,
        place_of,
        flat_ids,
        queries.reshape(row_blocks, tokens, width),
        passages,
        pos_index.reshape(row_blocks, 1, -1),
    )
    return (losses, query_grads[:, None], passage_grads[:, None])


def solution(mesh):
    in_specs = (
        P("dp", "cand", None, None),
        P("cand", None, None, None),
        P("dp", None),
        P("dp", None),
    )
    out_specs = (P("dp", "cand"), P("dp", "cand", None, None), P("cand", "dp", None, None))
    return jax.shard_map(
        functools.partial(on_device, mesh.shape["cand"], mesh.shape["dp"]),
        mesh=mesh,
        in_specs=in_specs,
        out_specs=out_specs,
        check_vma=False,
    )
```

```python
import functools
import math

import jax
import jax.numpy as jnp
from jax import lax
from jax.experimental import pallas as pl
from jax.experimental.pallas import tpu as pltpu
from jax.sharding import PartitionSpec as P

softness = 0.05
loss_scale = 32.0
to_exp2 = math.log2(math.e) / softness
MESH = pl.DeviceIdType.MESH
HIGHEST = lax.Precision.HIGHEST
LANES = 128
CODE_ROWS = 16
SCALE_STEPS = 256.0
TOP = 32700.0
TINY = 1e-30
GROUP = 32
CHUNK = 256


def to_codes(values):
    top = jnp.maximum(jnp.max(jnp.abs(values), 1), TINY)
    scale_code = jnp.ceil(SCALE_STEPS * (jnp.log2(top) - math.log2(TOP)))
    inverse = jnp.exp2(scale_code * (-1.0 / SCALE_STEPS))
    codes = jnp.round(values * inverse[:, None, :]).astype(jnp.int32).astype(jnp.int16)
    return codes, scale_code


def scale_of(scale_code):
    return jnp.exp2(scale_code * (1.0 / SCALE_STEPS))


def fill_tables(blocks_here, cap, ids_ref, table):
    count = ids_ref.shape[0] * ids_ref.shape[1]
    columns = ids_ref.shape[1]
    along = lax.broadcasted_iota(jnp.int32, (count, LANES), 1)
    down = lax.broadcasted_iota(jnp.int32, (count, LANES), 0)
    owner_along = jnp.full((count, LANES), -1, jnp.int32)
    owner_down = jnp.full((count, LANES), -1, jnp.int32)
    for request in range(count):
        owner = ids_ref[request // columns, request % columns] // blocks_here
        owner_along = jnp.where(along == request, owner, owner_along)
        owner_down = jnp.where(down == request, owner, owner_down)
    same = owner_along == owner_down
    rank_along = jnp.sum((same & (down < along)).astype(jnp.int32), 0, keepdims=True)
    place_along = owner_along[:1] * cap + rank_along
    rank_down = jnp.sum((same & (along < down)).astype(jnp.int32), 1, keepdims=True)
    here = owner_down * cap + rank_down == along
    request_along = jnp.sum(jnp.where(here, down + 1, 0), 0, keepdims=True) - 1
    row = lax.broadcasted_iota(jnp.int32, table.shape, 0)
    table[...] = jnp.where(row == 0, request_along, place_along)


def main_kernel(
    rows,
    ring,
    cap,
    ids_ref,
    q_ref,
    p_ref,
    pos_ref,
    loss_ref,
    query_out,
    passage_out,
    table,
    table_s,
    q_send,
    q_slot,
    q_turned,
    p_turned,
    high,
    low,
    totals,
    scores,
    grad_t,
    back_scales,
    back_out,
    back_in,
    acc,
    z_out,
    z_in,
    table_sem,
    send_sem,
    q_sem,
    score_sem,
    back_sem,
    z_send_sem,
    z_recv_sem,
):
    row_blocks, tokens, width = q_ref.shape
    blocks_here, per_block, passage_len, _ = p_ref.shape
    flat = rows * tokens
    chunk = min(CHUNK, flat)
    me = lax.axis_index("cand")
    plane = lax.axis_index("dp")
    half_blocks = blocks_here // 2
    groups = half_blocks * passage_len // GROUP
    values_here = half_blocks * passage_len
    tiles = tokens // CODE_ROWS

    def peer_of(offset):
        return lax.rem(me + offset, rows)

    barrier = pltpu.get_barrier_semaphore()

    def greet(offset, _):
        pl.semaphore_signal(
            barrier, inc=1, device_id={"cand": peer_of(offset)}, device_id_type=MESH
        )
        return 0

    lax.fori_loop(1, rows, greet, 0)
    up, down = lax.rem(plane + 1, ring), lax.rem(plane + ring - 1, ring)
    for neighbour in (up, down):
        pl.semaphore_signal(barrier, inc=1, device_id={"dp": neighbour}, device_id_type=MESH)

    fill_tables(blocks_here, cap, ids_ref, table)
    to_scalars = pltpu.make_async_copy(table, table_s, table_sem)
    to_scalars.start()
    to_scalars.wait()

    def request_at(place):
        return table_s[0, place]

    def place_of(request):
        return table_s[1, request]

    def fill(owner, _):
        for slot in range(cap):
            request = jnp.maximum(request_at(owner * cap + slot), 0)
            q_send[slot, owner] = q_ref[request // 2]
        return 0

    lax.fori_loop(0, rows, fill, 0)
    my_rows = pl.ds(pl.multiple_of(me * tokens, tokens), tokens)
    pl.semaphore_wait(barrier, rows - 1 + 2)

    def q_copy(slot, peer):
        return pltpu.make_async_remote_copy(
            src_ref=q_send.at[slot, peer],
            dst_ref=q_slot.at[slot, my_rows],
            send_sem=send_sem.at[0],
            recv_sem=q_sem.at[slot],
            device_id={"cand": peer},
            device_id_type=MESH,
        )

    for slot in range(cap):

        def send_queries(offset, _, slot=slot):
            q_copy(slot, peer_of(offset)).start()
            return 0

        lax.fori_loop(1, rows, send_queries, 0)
        q_slot[slot, my_rows] = q_send[slot, me]

    def turn_passage(c, _):
        for block in range(blocks_here):
            p_turned[block, c] = p_ref[block, c].T
        return 0

    lax.fori_loop(0, per_block, turn_passage, 0)

    head = pl.ds(0, flat - tokens)
    lane = lax.broadcasted_iota(jnp.int32, (flat, LANES), 1)
    query_of = lax.broadcasted_iota(jnp.int32, (flat, LANES), 0) // tokens
    my_scores = jnp.zeros((per_block, LANES), jnp.float32)

    def my_request(slot):
        return request_at(me * cap + slot)

    def my_block(slot):
        request = jnp.maximum(my_request(slot), 0)
        return ids_ref[request // 2, request % 2] % blocks_here

    def forward(slot, my_scores):
        pltpu.make_async_copy(q_slot.at[slot, head], q_slot.at[slot, head], q_sem.at[slot]).wait()
        block = my_block(slot)
        q_turned[slot] = q_slot[slot].T

        def candidate(c, _):
            passage = p_ref[block, c]
            for start in range(0, flat, chunk):
                here = pl.ds(start, chunk)
                similar = jnp.dot(
                    passage, q_turned[slot, :, here], preferred_element_type=jnp.float32
                )
                exponent = jnp.exp2(similar * to_exp2)
                rounded = exponent.astype(jnp.bfloat16)
                high[slot, c, :, here] = rounded
                low[slot, c, :, here] = (exponent - rounded.astype(jnp.float32)).astype(
                    jnp.bfloat16
                )
                totals[slot, pl.ds(c, 1), here] = jnp.sum(exponent, 0, keepdims=True)
            return 0

        lax.fori_loop(0, per_block, candidate, 0)
        soft_max = softness * jnp.log(totals[slot])
        place = (query_of + slot * rows == lane).astype(jnp.float32)
        return my_scores + jnp.dot(
            soft_max, place, precision=HIGHEST, preferred_element_type=jnp.float32
        )

    my_scores = lax.fori_loop(0, cap, forward, my_scores)
    scores[me] = my_scores

    def send_scores(offset, _):
        pltpu.make_async_remote_copy(
            src_ref=scores.at[me],
            dst_ref=scores.at[me],
            send_sem=send_sem.at[1],
            recv_sem=score_sem,
            device_id={"cand": peer_of(offset)},
            device_id_type=MESH,
        ).start()
        return 0

    lax.fori_loop(1, rows, send_scores, 0)
    others = pl.ds(0, rows - 1)
    pltpu.make_async_copy(scores.at[others], scores.at[others], score_sem).wait()

    lane_in = lax.broadcasted_iota(jnp.int32, (LANES, rows), 0)
    query_in = lax.broadcasted_iota(jnp.int32, (LANES, rows), 1)

    def scores_of(place):
        pick = (lane_in == query_in + (place % cap) * rows).astype(jnp.float32)
        return jnp.dot(
            scores[place // cap], pick, precision=HIGHEST, preferred_element_type=jnp.float32
        )

    column = lax.broadcasted_iota(jnp.int32, (per_block, rows), 0)
    spread = (
        lax.broadcasted_iota(jnp.int32, (rows, flat), 1) // tokens
        == lax.broadcasted_iota(jnp.int32, (rows, flat), 0)
    ).astype(jnp.float32)

    position_row = lax.broadcasted_iota(jnp.int32, pos_ref.shape, 0)

    def positives(block_row):
        return jnp.sum(jnp.where(position_row == block_row, pos_ref[...], 0), 0, keepdims=True)

    def factors(slot, _):
        request = my_request(slot)
        valid = jnp.where(request >= 0, loss_scale, 0.0)
        request = jnp.maximum(request, 0)
        block_row, half = request // 2, request % 2
        mine = scores_of(me * cap + slot)
        other = scores_of(place_of(block_row * 2 + 1 - half))
        log_total = jnp.log(
            jnp.sum(jnp.exp(mine), 0, keepdims=True) + jnp.sum(jnp.exp(other), 0, keepdims=True)
        )
        onehot = (column + half * per_block == positives(block_row)).astype(jnp.float32)
        dlogit = valid * (jnp.exp(mine - log_total) - onehot)
        wide = jnp.dot(dlogit, spread, precision=HIGHEST, preferred_element_type=jnp.float32)
        totals[slot] = wide / totals[slot]
        return 0

    lax.fori_loop(0, cap, factors, 0)

    plus, minus = ring // 2, ring - 1 - ring // 2
    chains = []
    first = 0
    for half, sign, length in ((0, 1, plus), (0, -1, minus), (1, 1, minus), (1, -1, plus)):
        chains.append((half, sign, length, first))
        first += length
    order = [
        ring // 2 - (k + 1) // 2 if k % 2 == 1 else k // 2 + ring // 2 for k in range(ring)
    ]

    def z_copy(chain, step):
        half, sign, length, first = chain
        return pltpu.make_async_remote_copy(
            src_ref=z_out.at[first + step],
            dst_ref=z_in.at[first + step],
            send_sem=z_send_sem.at[first + step],
            recv_sem=z_recv_sem.at[first + step],
            device_id={"dp": up if sign > 0 else down},
            device_id_type=MESH,
        )

    def own_part(c, half):
        part = acc[c, pl.ds(half * half_blocks, half_blocks)]
        return part.reshape(groups, GROUP, width)

    def z_received(chain, step):
        z_copy(chain, step).wait_recv()
        place = chain[3] + step
        codes = z_in[place, pl.ds(0, values_here)].astype(jnp.int32).astype(jnp.float32)
        scale_code = z_in[place, pl.ds(values_here, CODE_ROWS)].astype(jnp.int32)
        scale = scale_of(scale_code.astype(jnp.float32)[:groups])
        return codes.reshape(groups, GROUP, width) * scale[:, None, :]

    def z_hop(chain, step, c):
        part = own_part(c, chain[0])
        if step:
            part = part + z_received(chain, step - 1)
        codes, scale_code = to_codes(part)
        place = chain[3] + step
        z_out[place, pl.ds(0, values_here)] = codes.reshape(values_here, width)
        if groups < CODE_ROWS:
            scale_code = jnp.concatenate(
                [scale_code, jnp.zeros((CODE_ROWS - groups, width), jnp.float32)], 0
            )
        z_out[place, pl.ds(values_here, CODE_ROWS)] = scale_code.astype(jnp.int32).astype(
            jnp.int16
        )
        z_copy(chain, step).start()

    def query_gradient(slot):
        block = my_block(slot)
        grad_t[...] = jnp.zeros_like(grad_t)

        def candidate(c, _):
            passage = p_turned[block, c]
            for start in range(0, flat, chunk):
                here = pl.ds(start, chunk)
                product = jnp.dot(
                    passage, high[slot, c, :, here], preferred_element_type=jnp.float32
                ) + jnp.dot(passage, low[slot, c, :, here], preferred_element_type=jnp.float32)
                grad_t[:, here] += product * totals[slot, pl.ds(c, 1), here]
            return 0

        lax.fori_loop(0, per_block, candidate, 0)
        pieces = grad_t[...].T.reshape(rows, tokens, width)
        codes, scale_code = to_codes(pieces)
        for tile in range(tiles):
            back_out[:, slot * tiles + tile] = codes[:, tile * CODE_ROWS : (tile + 1) * CODE_ROWS]
        back_scales[slot] = scale_code

    def send_back(offset, _):
        peer = peer_of(offset)
        pltpu.make_async_remote_copy(
            src_ref=back_out.at[peer],
            dst_ref=back_in.at[me],
            send_sem=send_sem.at[2],
            recv_sem=back_sem,
            device_id={"cand": peer},
            device_id_type=MESH,
        ).start()
        return 0

    def start_back():
        filler = jnp.zeros((rows, width), jnp.float32)
        stacked = jnp.stack(
            [back_scales[k] if k < cap else filler for k in range(CODE_ROWS)], 1
        )
        back_out[:, cap * tiles] = stacked.astype(jnp.int32).astype(jnp.int16)
        lax.fori_loop(1, rows, send_back, 0)
        back_in[me] = back_out[me]

    def gradients(step, _):
        near = jnp.where(step % 2 == 1, ring // 2 - (step + 1) // 2, step // 2 + ring // 2)
        c = lax.rem(plane + near, ring)
        acc[c] = jnp.zeros(acc.shape[1:], jnp.float32)

        def one_slot(slot, _):
            block = my_block(slot)
            scaled = q_turned[slot].astype(jnp.float32) * totals[slot, pl.ds(c, 1)]
            scaled_high = scaled.astype(jnp.bfloat16)
            scaled_low = (scaled - scaled_high.astype(jnp.float32)).astype(jnp.bfloat16)
            both = jnp.concatenate([scaled_high, scaled_low], 0)
            along = (((1,), (1,)), ((), ()))
            first = lax.dot_general(
                high[slot, c], both, along, preferred_element_type=jnp.float32
            )
            passage_grad = (
                first[:, :width]
                + first[:, width:]
                + lax.dot_general(
                    low[slot, c], scaled_high, along, preferred_element_type=jnp.float32
                )
            )
            for local in range(blocks_here):
                chosen = jnp.where(block == local, 1.0, 0.0)
                acc[c, local] += chosen * passage_grad
            return 0

        lax.fori_loop(0, cap, one_slot, 0)
        for k in range(per_block):

            @pl.when(step == k)
            def _(k=k):
                for chain in chains:
                    half, sign, length, first = chain
                    for hop in range(length):
                        if (sign * (length - hop) - order[k]) % ring == 0:
                            z_hop(chain, hop, c)

        @pl.when(step < cap)
        def _():
            query_gradient(step)

        @pl.when(step == cap - 1)
        def _():
            start_back()

        return 0

    lax.fori_loop(0, per_block, gradients, 0)

    def loss_row(block_row, _):
        first = scores_of(place_of(2 * block_row))
        second = scores_of(place_of(2 * block_row + 1))
        log_total = jnp.log(
            jnp.sum(jnp.exp(first), 0, keepdims=True) + jnp.sum(jnp.exp(second), 0, keepdims=True)
        )
        positive = positives(block_row)
        chosen = jnp.sum(jnp.where(column == positive, first, 0.0), 0, keepdims=True) + jnp.sum(
            jnp.where(column + per_block == positive, second, 0.0), 0, keepdims=True
        )
        here = lax.broadcasted_iota(jnp.int32, (1, rows), 1) == me
        loss = jnp.sum(jnp.where(here, log_total - chosen, 0.0), 1, keepdims=True)
        loss_ref[pl.ds(block_row, 1)] = loss
        return 0

    lax.fori_loop(0, row_blocks, loss_row, 0)

    for half in range(2):
        result = own_part(plane, half)
        for chain in chains:
            if chain[0] == half and chain[2]:
                result = result + z_received(chain, chain[2] - 1)
        passage_out[pl.ds(half * half_blocks, half_blocks)] = result.reshape(
            half_blocks, passage_len, width
        )

    pltpu.make_async_copy(back_in.at[others], back_in.at[others], back_sem).wait()
    scale_row = lax.broadcasted_iota(jnp.int32, (CODE_ROWS, width), 0)

    def piece(place):
        owner, slot = place // cap, place % cap
        codes = [back_in[owner, slot * tiles + tile] for tile in range(tiles)]
        codes = jnp.concatenate([c.astype(jnp.int32) for c in codes], 0).astype(jnp.float32)
        scale_code = back_in[owner, cap * tiles].astype(jnp.int32)
        scale_code = jnp.sum(jnp.where(scale_row == slot, scale_code, 0), 0, keepdims=True)
        return codes * scale_of(scale_code.astype(jnp.float32))

    def add_pair(block_row, _):
        query_out[block_row] = piece(place_of(2 * block_row)) + piece(place_of(2 * block_row + 1))
        return 0

    lax.fori_loop(0, row_blocks, add_pair, 0)

    for slot in range(cap):
        pltpu.make_async_copy(q_slot.at[slot, head], q_slot.at[slot, head], send_sem.at[0]).wait()
    pltpu.make_async_copy(scores.at[others], scores.at[others], send_sem.at[1]).wait()
    pltpu.make_async_copy(back_in.at[others], back_in.at[others], send_sem.at[2]).wait()
    for chain in chains:
        for step in range(chain[2]):
            z_copy(chain, step).wait_send()


def finish_kernel(*refs):
    for source, target in zip(refs[:3], refs[3:]):
        target[...] = source[...]


def on_device(rows, ring, queries, passages, cand_ids, pos_index):
    row_blocks, _, tokens, width = queries.shape
    blocks_here, per_block, passage_len, _ = passages.shape
    requests = 2 * row_blocks
    cap = 4 * ((requests + rows - 1) // rows)
    flat = rows * tokens
    smem = pl.BlockSpec(memory_space=pltpu.SMEM)
    vmem = pl.BlockSpec(memory_space=pltpu.VMEM)
    half_blocks = blocks_here // 2
    hops = 2 * (ring - 1)
    f32, bf16, i16 = jnp.float32, jnp.bfloat16, jnp.int16
    out_shape = (
        jax.ShapeDtypeStruct((row_blocks, 1), f32),
        jax.ShapeDtypeStruct((row_blocks, tokens, width), f32),
        jax.ShapeDtypeStruct((blocks_here, passage_len, width), f32),
    )
    z_rows = half_blocks * passage_len + CODE_ROWS
    back_tiles = cap * tokens // CODE_ROWS + 1
    results = pl.pallas_call(
        functools.partial(main_kernel, rows, ring, cap),
        out_shape=out_shape,
        in_specs=[smem] + [vmem] * 3,
        out_specs=(vmem, vmem, vmem),
        scratch_shapes=[
            pltpu.VMEM((8, LANES), jnp.int32),
            pltpu.SMEM((8, LANES), jnp.int32),
            pltpu.VMEM((cap, rows, tokens, width), bf16),
            pltpu.VMEM((cap, flat, width), bf16),
            pltpu.VMEM((cap, width, flat), bf16),
            pltpu.VMEM((blocks_here, per_block, width, passage_len), bf16),
            pltpu.VMEM((cap, per_block, passage_len, flat), bf16),
            pltpu.VMEM((cap, per_block, passage_len, flat), bf16),
            pltpu.VMEM((cap, per_block, flat), f32),
            pltpu.VMEM((rows, per_block, LANES), f32),
            pltpu.VMEM((width, flat), f32),
            pltpu.VMEM((cap, rows, width), f32),
            pltpu.VMEM((rows, back_tiles, CODE_ROWS, width), i16),
            pltpu.VMEM((rows, back_tiles, CODE_ROWS, width), i16),
            pltpu.VMEM((per_block, blocks_here, passage_len, width), f32),
            pltpu.VMEM((hops, z_rows, width), i16),
            pltpu.VMEM((hops, z_rows, width), i16),
            pltpu.SemaphoreType.DMA,
            pltpu.SemaphoreType.DMA((3,)),
            pltpu.SemaphoreType.DMA((cap,)),
            pltpu.SemaphoreType.DMA,
            pltpu.SemaphoreType.DMA,
            pltpu.SemaphoreType.DMA((hops,)),
            pltpu.SemaphoreType.DMA((hops,)),
        ],
        compiler_params=pltpu.CompilerParams(
            collective_id=0, has_side_effects=True, vmem_limit_bytes=60 * 1024 * 1024
        ),
        name="late_interaction",
    )(
        cand_ids,
        queries.reshape(row_blocks, tokens, width),
        passages,
        pos_index,
    )
    losses, query_grads, passage_grads = pl.pallas_call(
        finish_kernel,
        out_shape=out_shape,
        in_specs=[vmem] * 3,
        out_specs=(vmem, vmem, vmem),
        name="results",
    )(*results)
    return (losses, query_grads[:, None], passage_grads[:, None])


def solution(mesh):
    in_specs = (
        P("dp", "cand", None, None),
        P("cand", None, None, None),
        P("dp", None),
        P("dp", None),
    )
    out_specs = (P("dp", "cand"), P("dp", "cand", None, None), P("cand", "dp", None, None))
    return jax.shard_map(
        functools.partial(on_device, mesh.shape["cand"], mesh.shape["dp"]),
        mesh=mesh,
        in_specs=in_specs,
        out_specs=out_specs,
        check_vma=False,
    )
```

```python
import functools
import math

import jax
import jax.numpy as jnp
from jax import lax
from jax.experimental import pallas as pl
from jax.experimental.pallas import tpu as pltpu
from jax.sharding import PartitionSpec as P

softness = 0.05
loss_scale = 32.0
to_exp2 = math.log2(math.e) / softness
MESH = pl.DeviceIdType.MESH
HIGHEST = lax.Precision.HIGHEST
LANES = 128
CODE_ROWS = 16
SCALE_STEPS = 256.0
TOP = 32700.0
TINY = 1e-30
GROUP = 32
CHUNK = 256


def to_codes(values):
    top = jnp.maximum(jnp.max(jnp.abs(values), 1), TINY)
    scale_code = jnp.ceil(SCALE_STEPS * (jnp.log2(top) - math.log2(TOP)))
    inverse = jnp.exp2(scale_code * (-1.0 / SCALE_STEPS))
    codes = jnp.round(values * inverse[:, None, :]).astype(jnp.int32).astype(jnp.int16)
    return codes, scale_code


def scale_of(scale_code):
    return jnp.exp2(scale_code * (1.0 / SCALE_STEPS))


def fill_tables(blocks_here, cap, ids_ref, table):
    count = ids_ref.shape[0] * ids_ref.shape[1]
    along = lax.broadcasted_iota(jnp.int32, (count, LANES), 1)
    down = lax.broadcasted_iota(jnp.int32, (count, LANES), 0)
    ids = jnp.concatenate([ids_ref[:, :1], ids_ref[:, 1:]], 0)
    ids_down = jnp.broadcast_to(ids, (count, LANES))
    owner_down = ids_down // blocks_here
    owner_along = jnp.sum(jnp.where(along == down, owner_down, 0), 0, keepdims=True)
    same = (owner_along == owner_down) & (along < count)
    rank_along = jnp.sum((same & (down < along)).astype(jnp.int32), 0, keepdims=True)
    place_along = owner_along * cap + rank_along
    rank_down = jnp.sum((same & (along < down)).astype(jnp.int32), 1, keepdims=True)
    here = owner_down * cap + rank_down == along
    request_along = jnp.sum(jnp.where(here, down + 1, 0), 0, keepdims=True) - 1
    block_along = jnp.sum(jnp.where(here, ids_down % blocks_here, 0), 0, keepdims=True)
    row = lax.broadcasted_iota(jnp.int32, table.shape, 0)
    table[...] = jnp.where(
        row == 0, request_along, jnp.where(row == 1, place_along, block_along)
    )


def main_kernel(
    rows,
    ring,
    cap,
    ids_ref,
    q_ref,
    p_ref,
    pos_ref,
    loss_ref,
    query_out,
    passage_out,
    table,
    table_s,
    q_send,
    q_slot,
    q_turned,
    p_turned,
    high,
    low,
    totals,
    scores,
    products,
    scaled_even,
    scaled_odd,
    grad_t,
    back_scales,
    back_out,
    back_in,
    acc,
    z_out,
    z_in,
    table_sem,
    send_sem,
    q_sem,
    score_sem,
    back_sem,
    z_send_sem,
    z_recv_sem,
):
    row_blocks, tokens, width = q_ref.shape
    blocks_here, per_block, passage_len, _ = p_ref.shape
    flat = rows * tokens
    chunk = min(CHUNK, flat)
    me = lax.axis_index("cand")
    plane = lax.axis_index("dp")
    half_blocks = blocks_here // 2
    groups = half_blocks * passage_len // GROUP
    values_here = half_blocks * passage_len
    tiles = tokens // CODE_ROWS
    group_slots = cap // 2

    def peer_of(offset):
        return lax.rem(me + offset, rows)

    barrier = pltpu.get_barrier_semaphore()

    def greet(offset, _):
        pl.semaphore_signal(
            barrier, inc=1, device_id={"cand": peer_of(offset)}, device_id_type=MESH
        )
        return 0

    lax.fori_loop(1, rows, greet, 0)
    up, down = lax.rem(plane + 1, ring), lax.rem(plane + ring - 1, ring)
    for neighbour in (up, down):
        pl.semaphore_signal(barrier, inc=1, device_id={"dp": neighbour}, device_id_type=MESH)

    fill_tables(blocks_here, cap, ids_ref, table)
    to_scalars = pltpu.make_async_copy(table, table_s, table_sem)
    to_scalars.start()
    to_scalars.wait()

    def request_at(place):
        return table_s[0, place]

    def place_of(request):
        return table_s[1, request]

    def fill(owner, _):
        for slot in range(cap):
            request = jnp.maximum(request_at(owner * cap + slot), 0)
            q_send[slot, owner] = q_ref[request % row_blocks]
        return 0

    lax.fori_loop(0, rows, fill, 0)
    my_rows = pl.ds(pl.multiple_of(me * tokens, tokens), tokens)
    pl.semaphore_wait(barrier, rows - 1 + 2)

    def q_copy(slot, peer):
        return pltpu.make_async_remote_copy(
            src_ref=q_send.at[slot, peer],
            dst_ref=q_slot.at[slot, my_rows],
            send_sem=send_sem.at[0],
            recv_sem=q_sem.at[slot],
            device_id={"cand": peer},
            device_id_type=MESH,
        )

    for slot in range(cap):

        def send_queries(offset, _, slot=slot):
            q_copy(slot, peer_of(offset)).start()
            return 0

        lax.fori_loop(1, rows, send_queries, 0)
        q_slot[slot, my_rows] = q_send[slot, me]

    def turn_passage(c, _):
        for block in range(blocks_here):
            p_turned[block, c] = p_ref[block, c].T
        return 0

    lax.fori_loop(0, per_block, turn_passage, 0)

    head = pl.ds(0, flat - tokens)
    lane = lax.broadcasted_iota(jnp.int32, (flat, LANES), 1)
    query_of = lax.broadcasted_iota(jnp.int32, (flat, LANES), 0) // tokens
    my_scores = jnp.zeros((per_block, LANES), jnp.float32)

    def my_request(slot):
        return request_at(me * cap + slot)

    def my_block(slot):
        return table_s[2, me * cap + slot]

    def forward(slot, my_scores):
        pltpu.make_async_copy(q_slot.at[slot, head], q_slot.at[slot, head], q_sem.at[slot]).wait()
        block = my_block(slot)
        q_turned[slot] = q_slot[slot].T

        for c in range(per_block):
            passage = p_ref[block, c]
            for start in range(0, flat, chunk):
                here = pl.ds(start, chunk)
                similar = jnp.dot(
                    passage, q_turned[slot, :, here], preferred_element_type=jnp.float32
                )
                exponent = jnp.exp2(similar * to_exp2)
                rounded = exponent.astype(jnp.bfloat16)
                high[slot, c, :, here] = rounded
                low[slot, c, :, here] = (exponent - rounded.astype(jnp.float32)).astype(
                    jnp.bfloat16
                )
                totals[slot, c : c + 1, here] = jnp.sum(exponent, 0, keepdims=True)
        soft_max = softness * jnp.log(totals[slot])
        place = (query_of + slot * rows == lane).astype(jnp.float32)
        return my_scores + jnp.dot(
            soft_max, place, precision=HIGHEST, preferred_element_type=jnp.float32
        )

    my_scores = lax.fori_loop(0, cap, forward, my_scores)
    scores[me] = my_scores

    def send_scores(offset, _):
        pltpu.make_async_remote_copy(
            src_ref=scores.at[me],
            dst_ref=scores.at[me],
            send_sem=send_sem.at[1],
            recv_sem=score_sem,
            device_id={"cand": peer_of(offset)},
            device_id_type=MESH,
        ).start()
        return 0

    lax.fori_loop(1, rows, send_scores, 0)
    early = products.shape[0]

    def product(slot, block, c, here):
        passage = p_turned[block, c]
        return jnp.dot(
            passage, high[slot, c, :, here], preferred_element_type=jnp.float32
        ) + jnp.dot(passage, low[slot, c, :, here], preferred_element_type=jnp.float32)

    def early_products(slot, _):
        block = my_block(slot)
        for c in range(per_block):
            for start in range(0, flat, chunk):
                here = pl.ds(start, chunk)
                products[slot, c, :, here] = product(slot, block, c, here)
        return 0

    lax.fori_loop(0, early, early_products, 0)
    others = pl.ds(0, rows - 1)
    pltpu.make_async_copy(scores.at[others], scores.at[others], score_sem).wait()

    lane_in = lax.broadcasted_iota(jnp.int32, (LANES, rows), 0)
    query_in = lax.broadcasted_iota(jnp.int32, (LANES, rows), 1)

    def scores_of(place):
        pick = (lane_in == query_in + (place % cap) * rows).astype(jnp.float32)
        return jnp.dot(
            scores[place // cap], pick, precision=HIGHEST, preferred_element_type=jnp.float32
        )

    column = lax.broadcasted_iota(jnp.int32, (per_block, rows), 0)
    spread = (
        lax.broadcasted_iota(jnp.int32, (rows, flat), 1) // tokens
        == lax.broadcasted_iota(jnp.int32, (rows, flat), 0)
    ).astype(jnp.float32)

    position_row = lax.broadcasted_iota(jnp.int32, pos_ref.shape, 0)

    def positives(block_row):
        return jnp.sum(jnp.where(position_row == block_row, pos_ref[...], 0), 0, keepdims=True)

    def factors(slot, _):
        request = my_request(slot)
        valid = jnp.where(request >= 0, loss_scale, 0.0)
        request = jnp.maximum(request, 0)
        block_row, half = request % row_blocks, request // row_blocks
        mine = scores_of(me * cap + slot)
        other = scores_of(place_of((1 - half) * row_blocks + block_row))
        log_total = jnp.log(
            jnp.sum(jnp.exp(mine), 0, keepdims=True) + jnp.sum(jnp.exp(other), 0, keepdims=True)
        )
        onehot = (column + half * per_block == positives(block_row)).astype(jnp.float32)
        dlogit = valid * (jnp.exp(mine - log_total) - onehot)
        wide = jnp.dot(dlogit, spread, precision=HIGHEST, preferred_element_type=jnp.float32)
        totals[slot] = wide / totals[slot]
        return 0

    lax.fori_loop(0, cap, factors, 0)

    plus, minus = ring // 2, ring - 1 - ring // 2
    chains = []
    first = 0
    for half, sign, length in ((0, 1, plus), (0, -1, minus), (1, 1, minus), (1, -1, plus)):
        chains.append((half, sign, length, first))
        first += length
    order = [
        ring // 2 - (k + 1) // 2 if k % 2 == 1 else k // 2 + ring // 2 for k in range(ring)
    ]

    def z_copy(chain, step):
        half, sign, length, first = chain
        return pltpu.make_async_remote_copy(
            src_ref=z_out.at[first + step],
            dst_ref=z_in.at[first + step],
            send_sem=z_send_sem.at[first + step],
            recv_sem=z_recv_sem.at[first + step],
            device_id={"dp": up if sign > 0 else down},
            device_id_type=MESH,
        )

    def own_part(half):
        part = acc[pl.ds(half * half_blocks, half_blocks)]
        return part.reshape(groups, GROUP, width)

    def z_received(chain, step):
        z_copy(chain, step).wait_recv()
        place = chain[3] + step
        codes = z_in[place, pl.ds(0, values_here)].astype(jnp.int32).astype(jnp.float32)
        scale_code = z_in[place, pl.ds(values_here, CODE_ROWS)].astype(jnp.int32)
        scale = scale_of(scale_code.astype(jnp.float32)[:groups])
        return codes.reshape(groups, GROUP, width) * scale[:, None, :]

    def z_hop(chain, step):
        part = own_part(chain[0])
        if step:
            part = part + z_received(chain, step - 1)
        codes, scale_code = to_codes(part)
        place = chain[3] + step
        z_out[place, pl.ds(0, values_here)] = codes.reshape(values_here, width)
        if groups < CODE_ROWS:
            scale_code = jnp.concatenate(
                [scale_code, jnp.zeros((CODE_ROWS - groups, width), jnp.float32)], 0
            )
        z_out[place, pl.ds(values_here, CODE_ROWS)] = scale_code.astype(jnp.int32).astype(
            jnp.int16
        )
        z_copy(chain, step).start()

    def code_pieces(slot):
        codes, scale_code = to_codes(grad_t[...].T.reshape(rows, tokens, width))
        group, inner = slot // group_slots, slot % group_slots
        for tile in range(tiles):
            back_out[group, :, inner * tiles + tile] = codes[
                :, tile * CODE_ROWS : (tile + 1) * CODE_ROWS
            ]
        back_scales[slot] = scale_code

    def early_gradient(slot, _):
        for start in range(0, flat, chunk):
            here = pl.ds(start, chunk)
            grad_t[:, here] = sum(
                products[slot, c, :, here] * totals[slot, c : c + 1, here]
                for c in range(per_block)
            )
        code_pieces(slot)
        return 0

    def late_gradient(slot, _):
        block = my_block(slot)
        for start in range(0, flat, chunk):
            here = pl.ds(start, chunk)
            grad_t[:, here] = sum(
                product(slot, block, c, here) * totals[slot, c : c + 1, here]
                for c in range(per_block)
            )
        code_pieces(slot)
        return 0

    def start_back(group):
        filler = jnp.zeros((rows, width), jnp.float32)
        stacked = jnp.stack(
            [
                back_scales[group * group_slots + k] if k < group_slots else filler
                for k in range(CODE_ROWS)
            ],
            1,
        )
        back_out[group, :, group_slots * tiles] = stacked.astype(jnp.int32).astype(jnp.int16)

        def send_back(offset, _):
            peer = peer_of(offset)
            pltpu.make_async_remote_copy(
                src_ref=back_out.at[group, peer],
                dst_ref=back_in.at[group, me],
                send_sem=send_sem.at[2 + group],
                recv_sem=back_sem.at[group],
                device_id={"cand": peer},
                device_id_type=MESH,
            ).start()
            return 0

        lax.fori_loop(1, rows, send_back, 0)
        back_in[group, me] = back_out[group, me]

    def passage_at(step):
        near = jnp.where(step % 2 == 1, ring // 2 - (step + 1) // 2, step // 2 + ring // 2)
        return lax.rem(plane + near, ring)

    def prepare(buffer, slot, c):
        value = q_turned[slot].astype(jnp.float32) * totals[slot, pl.ds(c, 1)]
        value_high = value.astype(jnp.bfloat16)
        buffer[:width] = value_high
        buffer[width:] = (value - value_high.astype(jnp.float32)).astype(jnp.bfloat16)

    prepare(scaled_even, 0, passage_at(0))

    def gradients(step, _):
        c = passage_at(step)
        sums = [0.0] * blocks_here
        for slot in range(cap):
            now, later = (
                (scaled_even, scaled_odd) if slot % 2 == 0 else (scaled_odd, scaled_even)
            )
            if slot < cap - 1:
                prepare(later, slot + 1, c)
            else:
                prepare(later, 0, passage_at(lax.rem(step + 1, per_block)))
            along = (((1,), (1,)), ((), ()))
            first = lax.dot_general(
                high[slot, c], now[...], along, preferred_element_type=jnp.float32
            )
            second = lax.dot_general(
                low[slot, c], now[:width], along, preferred_element_type=jnp.float32
            )
            passage_grad = first[:, :width] + first[:, width:] + second
            for local in range(blocks_here):
                chosen = jnp.where(my_block(slot) == local, 1.0, 0.0)
                sums[local] = sums[local] + chosen * passage_grad
        for local in range(blocks_here):
            acc[local] = sums[local]
        for k in range(per_block):

            @pl.when(step == k)
            def _(k=k):
                for chain in chains:
                    half, sign, length, first = chain
                    for hop in range(length):
                        if (sign * (length - hop) - order[k]) % ring == 0:
                            z_hop(chain, hop)

        @pl.when(step == 0)
        def _():
            lax.fori_loop(0, early, early_gradient, 0)
            start_back(0)

        @pl.when((step > 0) & (step <= cap - early))
        def _():
            late_gradient(early + step - 1, 0)

        @pl.when(step == cap - early)
        def _():
            start_back(1)

        return 0

    lax.fori_loop(0, per_block, gradients, 0)

    def loss_row(block_row, losses):
        first = scores_of(place_of(block_row))
        second = scores_of(place_of(row_blocks + block_row))
        log_total = jnp.log(
            jnp.sum(jnp.exp(first), 0, keepdims=True) + jnp.sum(jnp.exp(second), 0, keepdims=True)
        )
        positive = positives(block_row)
        chosen = jnp.sum(jnp.where(column == positive, first, 0.0), 0, keepdims=True) + jnp.sum(
            jnp.where(column + per_block == positive, second, 0.0), 0, keepdims=True
        )
        here = lax.broadcasted_iota(jnp.int32, (1, rows), 1) == me
        loss = jnp.sum(jnp.where(here, log_total - chosen, 0.0), 1, keepdims=True)
        return jnp.where(loss_lane == block_row, loss, losses)

    loss_lane = lax.broadcasted_iota(jnp.int32, (1, row_blocks), 1)
    loss_ref[...] = lax.fori_loop(
        0, row_blocks, loss_row, jnp.zeros((1, row_blocks), jnp.float32)
    )

    for half in range(2):
        result = own_part(half)
        for chain in chains:
            if chain[0] == half and chain[2]:
                result = result + z_received(chain, chain[2] - 1)
        passage_out[pl.ds(half * half_blocks, half_blocks)] = result.reshape(
            half_blocks, passage_len, width
        )

    for group in range(2):
        back_others = back_in.at[group, others]
        pltpu.make_async_copy(back_others, back_others, back_sem.at[group]).wait()
    scale_row = lax.broadcasted_iota(jnp.int32, (CODE_ROWS, width), 0)

    def piece(place):
        owner, slot = place // cap, place % cap
        group, inner = slot // group_slots, slot % group_slots
        codes = [back_in[group, owner, inner * tiles + tile] for tile in range(tiles)]
        codes = jnp.concatenate([c.astype(jnp.int32) for c in codes], 0).astype(jnp.float32)
        scale_code = back_in[group, owner, group_slots * tiles].astype(jnp.int32)
        scale_code = jnp.sum(jnp.where(scale_row == inner, scale_code, 0), 0, keepdims=True)
        return codes * scale_of(scale_code.astype(jnp.float32))

    def add_pair(block_row, _):
        second = place_of(row_blocks + block_row)
        query_out[block_row] = piece(place_of(block_row)) + piece(second)
        return 0

    lax.fori_loop(0, row_blocks, add_pair, 0)

    for slot in range(cap):
        pltpu.make_async_copy(q_slot.at[slot, head], q_slot.at[slot, head], send_sem.at[0]).wait()
    pltpu.make_async_copy(scores.at[others], scores.at[others], send_sem.at[1]).wait()
    for group in range(2):
        back_others = back_in.at[group, others]
        pltpu.make_async_copy(back_others, back_others, send_sem.at[2 + group]).wait()
    for chain in chains:
        for step in range(chain[2]):
            z_copy(chain, step).wait_send()


def finish_kernel(*refs):
    for source, target in zip(refs[:3], refs[3:]):
        target[...] = source[...]


def on_device(rows, ring, queries, passages, cand_ids, pos_index):
    row_blocks, _, tokens, width = queries.shape
    blocks_here, per_block, passage_len, _ = passages.shape
    requests = 2 * row_blocks
    cap = 4 * ((requests + rows - 1) // rows)
    flat = rows * tokens
    vmem = pl.BlockSpec(memory_space=pltpu.VMEM)
    half_blocks = blocks_here // 2
    hops = 2 * (ring - 1)
    f32, bf16, i16 = jnp.float32, jnp.bfloat16, jnp.int16
    out_shape = (
        jax.ShapeDtypeStruct((1, row_blocks), f32),
        jax.ShapeDtypeStruct((row_blocks, tokens, width), f32),
        jax.ShapeDtypeStruct((blocks_here, passage_len, width), f32),
    )
    z_rows = half_blocks * passage_len + CODE_ROWS
    back_tiles = cap // 2 * tokens // CODE_ROWS + 1
    results = pl.pallas_call(
        functools.partial(main_kernel, rows, ring, cap),
        out_shape=out_shape,
        in_specs=[vmem] * 4,
        out_specs=(vmem, vmem, vmem),
        scratch_shapes=[
            pltpu.VMEM((8, LANES), jnp.int32),
            pltpu.SMEM((8, LANES), jnp.int32),
            pltpu.VMEM((cap, rows, tokens, width), bf16),
            pltpu.VMEM((cap, flat, width), bf16),
            pltpu.VMEM((cap, width, flat), bf16),
            pltpu.VMEM((blocks_here, per_block, width, passage_len), bf16),
            pltpu.VMEM((cap, per_block, passage_len, flat), bf16),
            pltpu.VMEM((cap, per_block, passage_len, flat), bf16),
            pltpu.VMEM((cap, per_block, flat), f32),
            pltpu.VMEM((rows, per_block, LANES), f32),
            pltpu.VMEM((cap // 2, per_block, width, flat), f32),
            pltpu.VMEM((2 * width, flat), bf16),
            pltpu.VMEM((2 * width, flat), bf16),
            pltpu.VMEM((width, flat), f32),
            pltpu.VMEM((cap, rows, width), f32),
            pltpu.VMEM((2, rows, back_tiles, CODE_ROWS, width), i16),
            pltpu.VMEM((2, rows, back_tiles, CODE_ROWS, width), i16),
            pltpu.VMEM((blocks_here, passage_len, width), f32),
            pltpu.VMEM((hops, z_rows, width), i16),
            pltpu.VMEM((hops, z_rows, width), i16),
            pltpu.SemaphoreType.DMA,
            pltpu.SemaphoreType.DMA((4,)),
            pltpu.SemaphoreType.DMA((cap,)),
            pltpu.SemaphoreType.DMA,
            pltpu.SemaphoreType.DMA((2,)),
            pltpu.SemaphoreType.DMA((hops,)),
            pltpu.SemaphoreType.DMA((hops,)),
        ],
        compiler_params=pltpu.CompilerParams(
            collective_id=0, has_side_effects=True, vmem_limit_bytes=62 * 1024 * 1024
        ),
        name="late_interaction",
    )(
        cand_ids,
        queries.reshape(row_blocks, tokens, width),
        passages,
        pos_index,
    )
    losses, query_grads, passage_grads = pl.pallas_call(
        finish_kernel,
        out_shape=out_shape,
        in_specs=[vmem] * 3,
        out_specs=(vmem, vmem, vmem),
        name="results",
    )(*results)
    return (losses.reshape(row_blocks, 1), query_grads[:, None], passage_grads[:, None])


def solution(mesh):
    in_specs = (
        P("dp", "cand", None, None),
        P("cand", None, None, None),
        P("dp", None),
        P("dp", None),
    )
    out_specs = (P("dp", "cand"), P("dp", "cand", None, None), P("cand", "dp", None, None))
    return jax.shard_map(
        functools.partial(on_device, mesh.shape["cand"], mesh.shape["dp"]),
        mesh=mesh,
        in_specs=in_specs,
        out_specs=out_specs,
        check_vma=False,
    )
```

```python
import functools
import math

import jax
import jax.numpy as jnp
from jax import lax
from jax.experimental import pallas as pl
from jax.experimental.pallas import tpu as pltpu
from jax.sharding import PartitionSpec as P

softness = 0.05
loss_scale = 32.0
to_exp2 = math.log2(math.e) / softness
MESH = pl.DeviceIdType.MESH
HIGHEST = lax.Precision.HIGHEST
LANES = 128
CODE_ROWS = 16
SCALE_STEPS = 256.0
TOP = 32700.0
TINY = 1e-30
GROUP = 32
CHUNK = 256
Q_GROUP = 1
ACC_SLOTS = 4
SCHEDULES = {
    8: (
        ("A+0", "B-0", "e0"),
        ("B+0", "e1", "k0"),
        ("A-0", "A+1", "B-1"),
        ("l2",),
        ("B+1", "A-1"),
        ("l3", "k1", "A+2", "B-2"),
        ("B+2", "A-2", "A+3", "B-3"),
        (),
    ),
    4: (
        ("A+0", "B-0"),
        ("B+0", "e0", "e1", "k0"),
        ("A-0", "A+1", "B-1", "l2"),
        ("l3", "k1"),
    ),
}


def to_codes(values):
    top = jnp.maximum(jnp.max(jnp.abs(values), 1), TINY)
    scale_code = jnp.ceil(SCALE_STEPS * (jnp.log2(top) - math.log2(TOP)))
    inverse = jnp.exp2(scale_code * (-1.0 / SCALE_STEPS))
    codes = jnp.round(values * inverse[:, None, :]).astype(jnp.int32).astype(jnp.int16)
    return codes, scale_code


def scale_of(scale_code):
    return jnp.exp2(scale_code * (1.0 / SCALE_STEPS))


def fill_tables(blocks_here, cap, ids_ref, table):
    count = ids_ref.shape[0] * ids_ref.shape[1]
    along = lax.broadcasted_iota(jnp.int32, (count, LANES), 1)
    down = lax.broadcasted_iota(jnp.int32, (count, LANES), 0)
    row_blocks = ids_ref.shape[1]
    halves = [jnp.broadcast_to(ids_ref[h : h + 1], (row_blocks, row_blocks)) for h in range(2)]
    square = (row_blocks, row_blocks)
    diagonal = lax.broadcasted_iota(jnp.int32, square, 0) == lax.broadcasted_iota(
        jnp.int32, square, 1
    )
    columns = [jnp.sum(jnp.where(diagonal, half, 0), 1, keepdims=True) for half in halves]
    ids_down = jnp.broadcast_to(jnp.concatenate(columns, 0), (count, LANES))
    owner_down = ids_down // blocks_here
    owner_along = jnp.sum(jnp.where(along == down, owner_down, 0), 0, keepdims=True)
    same = (owner_along == owner_down) & (along < count)
    rank_along = jnp.sum((same & (down < along)).astype(jnp.int32), 0, keepdims=True)
    place_along = owner_along * cap + rank_along
    rank_down = jnp.sum((same & (along < down)).astype(jnp.int32), 1, keepdims=True)
    here = owner_down * cap + rank_down == along
    request_along = jnp.sum(jnp.where(here, down + 1, 0), 0, keepdims=True) - 1
    block_along = jnp.sum(jnp.where(here, ids_down % blocks_here, 0), 0, keepdims=True)
    row = lax.broadcasted_iota(jnp.int32, table.shape, 0)
    table[...] = jnp.where(
        row == 0, request_along, jnp.where(row == 1, place_along, block_along)
    )


def main_kernel(
    rows,
    ring,
    cap,
    ids_ref,
    q_ref,
    p_ref,
    pos_ref,
    loss_ref,
    query_out,
    passage_out,
    table,
    table_s,
    q_send,
    q_slot,
    q_turned,
    p_turned,
    high,
    low,
    totals,
    scores,
    products,
    scaled_even,
    scaled_odd,
    grad_t,
    back_scales,
    back_out,
    back_in,
    acc,
    z_out,
    z_in,
    table_sem,
    send_sem,
    q_sem,
    score_sem,
    back_sem,
    z_send_sem,
    z_recv_sem,
):
    row_blocks, tokens, width = q_ref.shape
    blocks_here, per_block, passage_len, _ = p_ref.shape
    flat = rows * tokens
    chunk = min(CHUNK, flat)
    me = lax.axis_index("cand")
    plane = lax.axis_index("dp")
    groups = passage_len // GROUP
    tiles = tokens // CODE_ROWS
    group_slots = cap // 2

    head = pl.ds(0, flat - tokens)
    q_group = q_send.shape[2]

    def peer_of(offset):
        return lax.rem(me + offset, rows)

    barrier = pltpu.get_barrier_semaphore()

    def greet(offset, _):
        pl.semaphore_signal(
            barrier, inc=1, device_id={"cand": peer_of(offset)}, device_id_type=MESH
        )
        return 0

    lax.fori_loop(1, rows, greet, 0)
    up, down = lax.rem(plane + 1, ring), lax.rem(plane + ring - 1, ring)
    for neighbour in (up, down):
        pl.semaphore_signal(barrier, inc=1, device_id={"dp": neighbour}, device_id_type=MESH)

    fill_tables(blocks_here, cap, ids_ref, table)
    to_scalars = pltpu.make_async_copy(table, table_s, table_sem)
    to_scalars.start()
    to_scalars.wait()

    def request_at(place):
        return table_s[0, place]

    def place_of(request):
        return table_s[1, request]

    def fill(owner, _):
        for slot in range(cap):
            request = jnp.maximum(request_at(owner * cap + slot), 0)
            q_send[slot // q_group, owner, slot % q_group] = q_ref[request % row_blocks]
        return 0

    lax.fori_loop(0, rows, fill, 0)
    my_rows = pl.ds(pl.multiple_of(me * tokens, tokens), tokens)
    pl.semaphore_wait(barrier, rows - 1 + 2)

    def send_group(group):
        slots = pl.ds(group * q_group, q_group)

        def send_queries(offset, _):
            peer = peer_of(offset)
            pltpu.make_async_remote_copy(
                src_ref=q_send.at[group, peer],
                dst_ref=q_slot.at[slots, my_rows],
                send_sem=send_sem.at[0],
                recv_sem=q_sem.at[group],
                device_id={"cand": peer},
                device_id_type=MESH,
            ).start()
            return 0

        lax.fori_loop(1, rows, send_queries, 0)

    def q_wait(group, sem):
        arrived = q_slot.at[pl.ds(group * q_group, q_group), head]
        pltpu.make_async_copy(arrived, arrived, sem).wait()

    for group in range(cap // q_group):
        send_group(group)
    for slot in range(cap):
        q_slot[slot, my_rows] = q_send[slot // q_group, me, slot % q_group]

    def turn_passage(c, _):
        for block in range(blocks_here):
            p_turned[block, c] = p_ref[block, c].T
        return 0

    lax.fori_loop(0, per_block, turn_passage, 0)

    lane = lax.broadcasted_iota(jnp.int32, (flat, LANES), 1)
    query_of = lax.broadcasted_iota(jnp.int32, (flat, LANES), 0) // tokens
    my_scores = jnp.zeros((per_block, LANES), jnp.float32)

    def my_request(slot):
        return request_at(me * cap + slot)

    def my_block(slot):
        return table_s[2, me * cap + slot]

    early = products.shape[0]

    def product(slot, block, c, here):
        passage = p_turned[block, c]
        return jnp.dot(
            passage, high[slot, c, :, here], preferred_element_type=jnp.float32
        ) + jnp.dot(passage, low[slot, c, :, here], preferred_element_type=jnp.float32)

    def early_products(slot, _):
        block = my_block(slot)
        for c in range(per_block):
            for start in range(0, flat, chunk):
                here = pl.ds(start, chunk)
                products[slot, c, :, here] = product(slot, block, c, here)
        return 0

    def forward(slot, my_scores):
        @pl.when(lax.rem(slot, q_group) == 0)
        def _():
            q_wait(slot // q_group, q_sem.at[slot // q_group])

        block = my_block(slot)
        q_turned[slot] = q_slot[slot].T

        for c in range(per_block):
            passage = p_ref[block, c]
            for start in range(0, flat, chunk):
                here = pl.ds(start, chunk)
                similar = jnp.dot(
                    passage, q_turned[slot, :, here], preferred_element_type=jnp.float32
                )
                exponent = jnp.exp2(similar * to_exp2)
                rounded = exponent.astype(jnp.bfloat16)
                high[slot, c, :, here] = rounded
                low[slot, c, :, here] = (exponent - rounded.astype(jnp.float32)).astype(
                    jnp.bfloat16
                )
                totals[slot, c : c + 1, here] = jnp.sum(exponent, 0, keepdims=True)
        soft_max = softness * jnp.log(totals[slot])
        @pl.when(slot == 0)
        def _():
            early_products(0, 0)

        place = (query_of + slot * rows == lane).astype(jnp.float32)
        return my_scores + jnp.dot(
            soft_max, place, precision=HIGHEST, preferred_element_type=jnp.float32
        )

    my_scores = lax.fori_loop(0, cap, forward, my_scores)
    scores[me] = my_scores

    def send_scores(offset, _):
        pltpu.make_async_remote_copy(
            src_ref=scores.at[me],
            dst_ref=scores.at[me],
            send_sem=send_sem.at[1],
            recv_sem=score_sem,
            device_id={"cand": peer_of(offset)},
            device_id_type=MESH,
        ).start()
        return 0

    lax.fori_loop(1, rows, send_scores, 0)
    lax.fori_loop(1, early, early_products, 0)
    others = pl.ds(0, rows - 1)
    pltpu.make_async_copy(scores.at[others], scores.at[others], score_sem).wait()

    lane_in = lax.broadcasted_iota(jnp.int32, (LANES, rows), 0)
    query_in = lax.broadcasted_iota(jnp.int32, (LANES, rows), 1)

    def scores_of(place):
        pick = (lane_in == query_in + (place % cap) * rows).astype(jnp.float32)
        return jnp.dot(
            scores[place // cap], pick, precision=HIGHEST, preferred_element_type=jnp.float32
        )

    column = lax.broadcasted_iota(jnp.int32, (per_block, rows), 0)
    spread = (
        lax.broadcasted_iota(jnp.int32, (rows, flat), 1) // tokens
        == lax.broadcasted_iota(jnp.int32, (rows, flat), 0)
    ).astype(jnp.float32)

    position_row = lax.broadcasted_iota(jnp.int32, pos_ref.shape, 0)

    def positives(block_row):
        return jnp.sum(jnp.where(position_row == block_row, pos_ref[...], 0), 0, keepdims=True)

    def factors(slot, _):
        request = my_request(slot)
        valid = jnp.where(request >= 0, loss_scale, 0.0)
        request = jnp.maximum(request, 0)
        block_row, half = request % row_blocks, request // row_blocks
        mine = scores_of(me * cap + slot)
        other = scores_of(place_of((1 - half) * row_blocks + block_row))
        log_total = jnp.log(
            jnp.sum(jnp.exp(mine), 0, keepdims=True) + jnp.sum(jnp.exp(other), 0, keepdims=True)
        )
        onehot = (column + half * per_block == positives(block_row)).astype(jnp.float32)
        dlogit = valid * (jnp.exp(mine - log_total) - onehot)
        wide = jnp.dot(dlogit, spread, precision=HIGHEST, preferred_element_type=jnp.float32)
        totals[slot] = wide / totals[slot]
        return 0

    lax.fori_loop(0, cap, factors, 0, unroll=True)

    plus, minus = ring // 2, ring - 1 - ring // 2
    chains = []
    first = 0
    for local in range(blocks_here):
        kind = "A" if local < blocks_here // 2 else "B"
        for sign, length in ((1, plus), (-1, minus)) if kind == "A" else ((1, minus), (-1, plus)):
            chains.append((local, sign, length, first, kind + ("+" if sign > 0 else "-")))
            first += length
    order = [
        ring // 2 - (k + 1) // 2 if k % 2 == 1 else k // 2 + ring // 2 for k in range(ring)
    ]

    def z_copy(chain, step):
        _, sign, length, first, _ = chain
        return pltpu.make_async_remote_copy(
            src_ref=z_out.at[first + step],
            dst_ref=z_in.at[first + step],
            send_sem=z_send_sem.at[first + step],
            recv_sem=z_recv_sem.at[first + step],
            device_id={"dp": up if sign > 0 else down},
            device_id_type=MESH,
        )

    def ready(chain, hop):
        _, sign, length, _, _ = chain
        return [offset % ring for offset in order].index(sign * (length - hop) % ring)

    def own_part(local, step):
        return acc[step % ACC_SLOTS, local].reshape(groups, GROUP, width)

    def z_received(chain, step):
        z_copy(chain, step).wait_recv()
        place = chain[3] + step
        codes = z_in[place, pl.ds(0, passage_len)].astype(jnp.int32).astype(jnp.float32)
        scale_code = z_in[place, pl.ds(passage_len, CODE_ROWS)].astype(jnp.int32)
        scale = scale_of(scale_code.astype(jnp.float32)[:groups])
        return codes.reshape(groups, GROUP, width) * scale[:, None, :]

    def z_hop(chain, step):
        part = own_part(chain[0], ready(chain, step))
        if step:
            part = part + z_received(chain, step - 1)
        codes, scale_code = to_codes(part)
        place = chain[3] + step
        z_out[place, pl.ds(0, passage_len)] = codes.reshape(passage_len, width)
        if groups < CODE_ROWS:
            scale_code = jnp.concatenate(
                [scale_code, jnp.zeros((CODE_ROWS - groups, width), jnp.float32)], 0
            )
        z_out[place, pl.ds(passage_len, CODE_ROWS)] = scale_code.astype(jnp.int32).astype(
            jnp.int16
        )
        z_copy(chain, step).start()

    def code_pieces(slot):
        codes, scale_code = to_codes(grad_t[...].T.reshape(rows, tokens, width))
        group, inner = slot // group_slots, slot % group_slots
        for tile in range(tiles):
            back_out[group, :, inner * tiles + tile] = codes[
                :, tile * CODE_ROWS : (tile + 1) * CODE_ROWS
            ]
        back_scales[slot] = scale_code

    def early_gradient(slot, _):
        for start in range(0, flat, chunk):
            here = pl.ds(start, chunk)
            grad_t[:, here] = sum(
                products[slot, c, :, here] * totals[slot, c : c + 1, here]
                for c in range(per_block)
            )
        code_pieces(slot)
        return 0

    def late_gradient(slot, _):
        block = my_block(slot)
        for start in range(0, flat, chunk):
            here = pl.ds(start, chunk)
            grad_t[:, here] = sum(
                product(slot, block, c, here) * totals[slot, c : c + 1, here]
                for c in range(per_block)
            )
        code_pieces(slot)
        return 0

    def start_back(group):
        filler = jnp.zeros((rows, width), jnp.float32)
        stacked = jnp.stack(
            [
                back_scales[group * group_slots + k] if k < group_slots else filler
                for k in range(CODE_ROWS)
            ],
            1,
        )
        back_out[group, :, group_slots * tiles] = stacked.astype(jnp.int32).astype(jnp.int16)

        def send_back(offset, _):
            peer = peer_of(offset)
            pltpu.make_async_remote_copy(
                src_ref=back_out.at[group, peer],
                dst_ref=back_in.at[group, me],
                send_sem=send_sem.at[2 + group],
                recv_sem=back_sem.at[group],
                device_id={"cand": peer},
                device_id_type=MESH,
            ).start()
            return 0

        lax.fori_loop(1, rows, send_back, 0)
        back_in[group, me] = back_out[group, me]

    def passage_at(step):
        near = jnp.where(step % 2 == 1, ring // 2 - (step + 1) // 2, step // 2 + ring // 2)
        return lax.rem(plane + near, ring)

    def prepare(buffer, slot, c):
        value = q_turned[slot].astype(jnp.float32) * totals[slot, pl.ds(c, 1)]
        value_high = value.astype(jnp.bfloat16)
        buffer[:width] = value_high
        buffer[width:] = (value - value_high.astype(jnp.float32)).astype(jnp.bfloat16)

    prepare(scaled_even, 0, passage_at(0))

    def gradients(step, _):
        c = passage_at(step)
        sums = [0.0] * blocks_here
        for slot in range(cap):
            now, later = (
                (scaled_even, scaled_odd) if slot % 2 == 0 else (scaled_odd, scaled_even)
            )
            if slot < cap - 1:
                prepare(later, slot + 1, c)
            else:
                prepare(later, 0, passage_at(lax.rem(step + 1, per_block)))
            along = (((1,), (1,)), ((), ()))
            first = lax.dot_general(
                high[slot, c], now[...], along, preferred_element_type=jnp.float32
            )
            second = lax.dot_general(
                low[slot, c], now[:width], along, preferred_element_type=jnp.float32
            )
            passage_grad = first[:, :width] + first[:, width:] + second
            for local in range(blocks_here):
                chosen = jnp.where(my_block(slot) == local, 1.0, 0.0)
                sums[local] = sums[local] + chosen * passage_grad
        for local in range(blocks_here):
            acc[step % ACC_SLOTS, local] = sums[local]

        for k, actions in enumerate(SCHEDULES[ring]):
            if actions:

                @pl.when(step == k)
                def _(actions=actions):
                    for action in actions:
                        act(action)

        return 0

    def act(action):
        kind, number = action[:-1], int(action[-1])
        if kind == "e":
            early_gradient(number, 0)
        elif kind == "l":
            late_gradient(number, 0)
        elif kind == "k":
            start_back(number)
        else:
            for chain in chains:
                if chain[4] == kind:
                    z_hop(chain, number)

    lax.fori_loop(0, per_block, gradients, 0)

    lane_at = lax.broadcasted_iota(jnp.int32, (per_block, LANES), 1)
    request_lane = lax.broadcasted_iota(jnp.int32, (per_block, 2 * row_blocks), 1)
    logits = jnp.zeros((per_block, 2 * row_blocks), jnp.float32)
    for request in range(2 * row_blocks):
        place = place_of(request)
        mine = lane_at == (place % cap) * rows + me
        value = jnp.sum(jnp.where(mine, scores[place // cap], 0.0), 1, keepdims=True)
        logits = jnp.where(request_lane == request, value, logits)
    first, second = logits[:, :row_blocks], logits[:, row_blocks:]
    log_total = jnp.log(
        jnp.sum(jnp.exp(first), 0, keepdims=True) + jnp.sum(jnp.exp(second), 0, keepdims=True)
    )
    square = (row_blocks, row_blocks)
    diagonal = lax.broadcasted_iota(jnp.int32, square, 0) == lax.broadcasted_iota(
        jnp.int32, square, 1
    )
    my_column = lax.broadcasted_iota(jnp.int32, pos_ref.shape, 1) == me
    positive = jnp.sum(jnp.where(my_column, pos_ref[...], 0), 1, keepdims=True)
    positive = jnp.sum(jnp.where(diagonal, positive, 0), 0, keepdims=True)
    candidate = lax.broadcasted_iota(jnp.int32, (per_block, row_blocks), 0)
    chosen = jnp.where(candidate == positive, first, 0.0) + jnp.where(
        candidate + per_block == positive, second, 0.0
    )
    loss_ref[...] = log_total - jnp.sum(chosen, 0, keepdims=True)

    for local in range(blocks_here):
        result = own_part(local, per_block - 1)
        for chain in chains:
            if chain[0] == local and chain[2]:
                result = result + z_received(chain, chain[2] - 1)
        passage_out[local] = result.reshape(passage_len, width)

    for group in range(2):
        back_others = back_in.at[group, others]
        pltpu.make_async_copy(back_others, back_others, back_sem.at[group]).wait()
    scale_row = lax.broadcasted_iota(jnp.int32, (CODE_ROWS, width), 0)

    def piece(place):
        owner, slot = place // cap, place % cap
        group, inner = slot // group_slots, slot % group_slots
        codes = [back_in[group, owner, inner * tiles + tile] for tile in range(tiles)]
        codes = jnp.concatenate([c.astype(jnp.int32) for c in codes], 0).astype(jnp.float32)
        scale_code = back_in[group, owner, group_slots * tiles].astype(jnp.int32)
        scale_code = jnp.sum(jnp.where(scale_row == inner, scale_code, 0), 0, keepdims=True)
        return codes * scale_of(scale_code.astype(jnp.float32))

    def add_pair(block_row, _):
        second = place_of(row_blocks + block_row)
        query_out[block_row] = piece(place_of(block_row)) + piece(second)
        return 0

    lax.fori_loop(0, row_blocks, add_pair, 0)

    for group in range(cap // q_group):
        q_wait(group, send_sem.at[0])
    pltpu.make_async_copy(scores.at[others], scores.at[others], send_sem.at[1]).wait()
    for group in range(2):
        back_others = back_in.at[group, others]
        pltpu.make_async_copy(back_others, back_others, send_sem.at[2 + group]).wait()
    for chain in chains:
        for step in range(chain[2]):
            z_copy(chain, step).wait_send()


def finish_kernel(*refs):
    for source, target in zip(refs[:3], refs[3:]):
        target[...] = source[...]


def on_device(rows, ring, queries, passages, cand_ids, pos_index):
    row_blocks, _, tokens, width = queries.shape
    blocks_here, per_block, passage_len, _ = passages.shape
    requests = 2 * row_blocks
    cap = 4 * ((requests + rows - 1) // rows)
    flat = rows * tokens
    vmem = pl.BlockSpec(memory_space=pltpu.VMEM)
    hops = blocks_here * (ring - 1)
    f32, bf16, i16 = jnp.float32, jnp.bfloat16, jnp.int16
    out_shape = (
        jax.ShapeDtypeStruct((1, row_blocks), f32),
        jax.ShapeDtypeStruct((row_blocks, tokens, width), f32),
        jax.ShapeDtypeStruct((blocks_here, passage_len, width), f32),
    )
    z_rows = passage_len + CODE_ROWS
    back_tiles = cap // 2 * tokens // CODE_ROWS + 1
    results = pl.pallas_call(
        functools.partial(main_kernel, rows, ring, cap),
        out_shape=out_shape,
        in_specs=[vmem] * 4,
        out_specs=(vmem, vmem, vmem),
        scratch_shapes=[
            pltpu.VMEM((8, LANES), jnp.int32),
            pltpu.SMEM((8, LANES), jnp.int32),
            pltpu.VMEM((cap // Q_GROUP, rows, Q_GROUP, tokens, width), bf16),
            pltpu.VMEM((cap, flat, width), bf16),
            pltpu.VMEM((cap, width, flat), bf16),
            pltpu.VMEM((blocks_here, per_block, width, passage_len), bf16),
            pltpu.VMEM((cap, per_block, passage_len, flat), bf16),
            pltpu.VMEM((cap, per_block, passage_len, flat), bf16),
            pltpu.VMEM((cap, per_block, flat), f32),
            pltpu.VMEM((rows, per_block, LANES), f32),
            pltpu.VMEM((cap // 2, per_block, width, flat), f32),
            pltpu.VMEM((2 * width, flat), bf16),
            pltpu.VMEM((2 * width, flat), bf16),
            pltpu.VMEM((width, flat), f32),
            pltpu.VMEM((cap, rows, width), f32),
            pltpu.VMEM((2, rows, back_tiles, CODE_ROWS, width), i16),
            pltpu.VMEM((2, rows, back_tiles, CODE_ROWS, width), i16),
            pltpu.VMEM((ACC_SLOTS, blocks_here, passage_len, width), f32),
            pltpu.VMEM((hops, z_rows, width), i16),
            pltpu.VMEM((hops, z_rows, width), i16),
            pltpu.SemaphoreType.DMA,
            pltpu.SemaphoreType.DMA((4,)),
            pltpu.SemaphoreType.DMA((cap // Q_GROUP,)),
            pltpu.SemaphoreType.DMA,
            pltpu.SemaphoreType.DMA((2,)),
            pltpu.SemaphoreType.DMA((hops,)),
            pltpu.SemaphoreType.DMA((hops,)),
        ],
        compiler_params=pltpu.CompilerParams(
            collective_id=0, has_side_effects=True, vmem_limit_bytes=62 * 1024 * 1024
        ),
        name="late_interaction",
    )(
        cand_ids.T,
        queries.reshape(row_blocks, tokens, width),
        passages,
        pos_index,
    )
    losses, query_grads, passage_grads = pl.pallas_call(
        finish_kernel,
        out_shape=out_shape,
        in_specs=[vmem] * 3,
        out_specs=(vmem, vmem, vmem),
        name="results",
    )(*results)
    return (losses.reshape(row_blocks, 1), query_grads[:, None], passage_grads[:, None])


def solution(mesh):
    in_specs = (
        P("dp", "cand", None, None),
        P("cand", None, None, None),
        P("dp", None),
        P("dp", None),
    )
    out_specs = (P("dp", "cand"), P("dp", "cand", None, None), P("cand", "dp", None, None))
    return jax.shard_map(
        functools.partial(on_device, mesh.shape["cand"], mesh.shape["dp"]),
        mesh=mesh,
        in_specs=in_specs,
        out_specs=out_specs,
        check_vma=False,
    )
```

```python
import functools
import math

import jax
import jax.numpy as jnp
from jax import lax
from jax.experimental import pallas as pl
from jax.experimental.pallas import tpu as pltpu
from jax.sharding import PartitionSpec as P

softness = 0.05
loss_scale = 32.0
to_exp2 = math.log2(math.e) / softness
MESH = pl.DeviceIdType.MESH
HIGHEST = lax.Precision.HIGHEST
LANES = 128
CODE_ROWS = 16
SCALE_STEPS = 256.0
TOP = 32700.0
TINY = 1e-30
GROUP = 32
CHUNK = 256
Q_GROUP = 1
ACC_SLOTS = 3
SCHEDULES = {
    8: (
        ("A+0", "B-0"),
        ("B+0", "e0"),
        ("A-0", "e1", "k0", "A+1", "B-1"),
        ("e2",),
        ("B+1", "A-1"),
        ("l3", "k1", "A+2", "B-2"),
        ("B+2", "A-2", "A+3", "B-3"),
        (),
    ),
    4: (
        ("A+0", "B-0"),
        ("B+0", "e0", "e1", "k0"),
        ("A-0", "A+1", "B-1", "l2"),
        ("l3", "k1"),
    ),
}


def to_codes(values):
    top = jnp.maximum(jnp.max(jnp.abs(values), 1), TINY)
    scale_code = jnp.ceil(SCALE_STEPS * (jnp.log2(top) - math.log2(TOP)))
    inverse = jnp.exp2(scale_code * (-1.0 / SCALE_STEPS))
    codes = jnp.round(values * inverse[:, None, :]).astype(jnp.int32).astype(jnp.int16)
    return codes, scale_code


def scale_of(scale_code):
    return jnp.exp2(scale_code * (1.0 / SCALE_STEPS))


def fill_tables(blocks_here, cap, ids_ref, table):
    count = ids_ref.shape[0] * ids_ref.shape[1]
    along = lax.broadcasted_iota(jnp.int32, (count, LANES), 1)
    down = lax.broadcasted_iota(jnp.int32, (count, LANES), 0)
    row_blocks = ids_ref.shape[1]
    halves = [jnp.broadcast_to(ids_ref[h : h + 1], (row_blocks, row_blocks)) for h in range(2)]
    square = (row_blocks, row_blocks)
    diagonal = lax.broadcasted_iota(jnp.int32, square, 0) == lax.broadcasted_iota(
        jnp.int32, square, 1
    )
    columns = [jnp.sum(jnp.where(diagonal, half, 0), 1, keepdims=True) for half in halves]
    ids_down = jnp.broadcast_to(jnp.concatenate(columns, 0), (count, LANES))
    owner_down = ids_down // blocks_here
    owner_along = jnp.sum(jnp.where(along == down, owner_down, 0), 0, keepdims=True)
    same = (owner_along == owner_down) & (along < count)
    rank_along = jnp.sum((same & (down < along)).astype(jnp.int32), 0, keepdims=True)
    place_along = owner_along * cap + rank_along
    rank_down = jnp.sum((same & (along < down)).astype(jnp.int32), 1, keepdims=True)
    here = owner_down * cap + rank_down == along
    request_along = jnp.sum(jnp.where(here, down + 1, 0), 0, keepdims=True) - 1
    block_along = jnp.sum(jnp.where(here, ids_down % blocks_here, 0), 0, keepdims=True)
    row = lax.broadcasted_iota(jnp.int32, table.shape, 0)
    table[...] = jnp.where(
        row == 0, request_along, jnp.where(row == 1, place_along, block_along)
    )


def main_kernel(
    rows,
    ring,
    cap,
    ids_ref,
    q_ref,
    p_ref,
    pos_ref,
    loss_ref,
    query_out,
    passage_out,
    table,
    table_s,
    q_send,
    q_slot,
    q_turned,
    p_turned,
    high,
    low,
    totals,
    scores,
    products,
    scaled_even,
    scaled_odd,
    grad_t,
    back_scales,
    back_out,
    back_in,
    acc,
    z_out,
    z_in,
    table_sem,
    send_sem,
    q_sem,
    score_sem,
    back_sem,
    z_send_sem,
    z_recv_sem,
):
    row_blocks, tokens, width = q_ref.shape
    blocks_here, per_block, passage_len, _ = p_ref.shape
    flat = rows * tokens
    chunk = min(CHUNK, flat)
    me = lax.axis_index("cand")
    plane = lax.axis_index("dp")
    groups = passage_len // GROUP
    tiles = tokens // CODE_ROWS
    group_slots = cap // 2

    head = pl.ds(0, flat - tokens)
    q_group = q_send.shape[2]

    def peer_of(offset):
        return lax.rem(me + offset, rows)

    barrier = pltpu.get_barrier_semaphore()

    def greet(offset, _):
        pl.semaphore_signal(
            barrier, inc=1, device_id={"cand": peer_of(offset)}, device_id_type=MESH
        )
        return 0

    lax.fori_loop(1, rows, greet, 0)
    up, down = lax.rem(plane + 1, ring), lax.rem(plane + ring - 1, ring)
    for neighbour in (up, down):
        pl.semaphore_signal(barrier, inc=1, device_id={"dp": neighbour}, device_id_type=MESH)

    fill_tables(blocks_here, cap, ids_ref, table)
    to_scalars = pltpu.make_async_copy(table, table_s, table_sem)
    to_scalars.start()
    to_scalars.wait()

    def request_at(place):
        return table_s[0, place]

    def place_of(request):
        return table_s[1, request]

    def fill(owner, _):
        for slot in range(cap):
            request = jnp.maximum(request_at(owner * cap + slot), 0)
            q_send[slot // q_group, owner, slot % q_group] = q_ref[request % row_blocks]
        return 0

    lax.fori_loop(0, rows, fill, 0)
    my_rows = pl.ds(pl.multiple_of(me * tokens, tokens), tokens)
    pl.semaphore_wait(barrier, rows - 1 + 2)

    def send_group(group):
        slots = pl.ds(group * q_group, q_group)

        def send_queries(offset, _):
            peer = peer_of(offset)
            pltpu.make_async_remote_copy(
                src_ref=q_send.at[group, peer],
                dst_ref=q_slot.at[slots, my_rows],
                send_sem=send_sem.at[0],
                recv_sem=q_sem.at[group],
                device_id={"cand": peer},
                device_id_type=MESH,
            ).start()
            return 0

        lax.fori_loop(1, rows, send_queries, 0)

    def q_wait(group, sem):
        arrived = q_slot.at[pl.ds(group * q_group, q_group), head]
        pltpu.make_async_copy(arrived, arrived, sem).wait()

    for group in range(cap // q_group):
        send_group(group)
    for slot in range(cap):
        q_slot[slot, my_rows] = q_send[slot // q_group, me, slot % q_group]

    def turn_passage(c, _):
        for block in range(blocks_here):
            p_turned[block, c] = p_ref[block, c].T
        return 0

    lax.fori_loop(0, per_block, turn_passage, 0)

    lane = lax.broadcasted_iota(jnp.int32, (flat, LANES), 1)
    query_of = lax.broadcasted_iota(jnp.int32, (flat, LANES), 0) // tokens
    my_scores = jnp.zeros((per_block, LANES), jnp.float32)

    def my_request(slot):
        return request_at(me * cap + slot)

    def my_block(slot):
        return table_s[2, me * cap + slot]

    early = products.shape[0]

    def product(slot, block, c, here):
        passage = p_turned[block, c]
        return jnp.dot(
            passage, high[slot, c, :, here], preferred_element_type=jnp.float32
        ) + jnp.dot(passage, low[slot, c, :, here], preferred_element_type=jnp.float32)

    def early_products(slot, _):
        block = my_block(slot)
        for c in range(per_block):
            for start in range(0, flat, chunk):
                here = pl.ds(start, chunk)
                products[slot, c, :, here] = product(slot, block, c, here)
        return 0

    def forward(slot, my_scores):
        @pl.when(lax.rem(slot, q_group) == 0)
        def _():
            q_wait(slot // q_group, q_sem.at[slot // q_group])

        block = my_block(slot)
        q_turned[slot] = q_slot[slot].T

        for c in range(per_block):
            passage = p_ref[block, c]
            for start in range(0, flat, chunk):
                here = pl.ds(start, chunk)
                similar = jnp.dot(
                    passage, q_turned[slot, :, here], preferred_element_type=jnp.float32
                )
                exponent = jnp.exp2(similar * to_exp2)
                rounded = exponent.astype(jnp.bfloat16)
                high[slot, c, :, here] = rounded
                low[slot, c, :, here] = (exponent - rounded.astype(jnp.float32)).astype(
                    jnp.bfloat16
                )
                totals[slot, c : c + 1, here] = jnp.sum(exponent, 0, keepdims=True)
        soft_max = softness * jnp.log(totals[slot])
        @pl.when(slot == 0)
        def _():
            early_products(0, 0)

        place = (query_of + slot * rows == lane).astype(jnp.float32)
        return my_scores + jnp.dot(
            soft_max, place, precision=HIGHEST, preferred_element_type=jnp.float32
        )

    my_scores = lax.fori_loop(0, cap, forward, my_scores)
    scores[me] = my_scores

    def send_scores(offset, _):
        pltpu.make_async_remote_copy(
            src_ref=scores.at[me],
            dst_ref=scores.at[me],
            send_sem=send_sem.at[1],
            recv_sem=score_sem,
            device_id={"cand": peer_of(offset)},
            device_id_type=MESH,
        ).start()
        return 0

    lax.fori_loop(1, rows, send_scores, 0)
    lax.fori_loop(1, early, early_products, 0)
    others = pl.ds(0, rows - 1)
    pltpu.make_async_copy(scores.at[others], scores.at[others], score_sem).wait()

    lane_in = lax.broadcasted_iota(jnp.int32, (LANES, rows), 0)
    query_in = lax.broadcasted_iota(jnp.int32, (LANES, rows), 1)

    def scores_of(place):
        pick = (lane_in == query_in + (place % cap) * rows).astype(jnp.float32)
        return jnp.dot(
            scores[place // cap], pick, precision=HIGHEST, preferred_element_type=jnp.float32
        )

    column = lax.broadcasted_iota(jnp.int32, (per_block, rows), 0)
    spread = (
        lax.broadcasted_iota(jnp.int32, (rows, flat), 1) // tokens
        == lax.broadcasted_iota(jnp.int32, (rows, flat), 0)
    ).astype(jnp.float32)

    position_row = lax.broadcasted_iota(jnp.int32, pos_ref.shape, 0)

    def positives(block_row):
        return jnp.sum(jnp.where(position_row == block_row, pos_ref[...], 0), 0, keepdims=True)

    def factors(slot, _):
        request = my_request(slot)
        valid = jnp.where(request >= 0, loss_scale, 0.0)
        request = jnp.maximum(request, 0)
        block_row, half = request % row_blocks, request // row_blocks
        mine = scores_of(me * cap + slot)
        other = scores_of(place_of((1 - half) * row_blocks + block_row))
        log_total = jnp.log(
            jnp.sum(jnp.exp(mine), 0, keepdims=True) + jnp.sum(jnp.exp(other), 0, keepdims=True)
        )
        onehot = (column + half * per_block == positives(block_row)).astype(jnp.float32)
        dlogit = valid * (jnp.exp(mine - log_total) - onehot)
        wide = jnp.dot(dlogit, spread, precision=HIGHEST, preferred_element_type=jnp.float32)
        totals[slot] = wide / totals[slot]
        return 0

    lax.fori_loop(0, cap, factors, 0, unroll=True)

    plus, minus = ring // 2, ring - 1 - ring // 2
    chains = []
    first = 0
    for local in range(blocks_here):
        kind = "A" if local < blocks_here // 2 else "B"
        for sign, length in ((1, plus), (-1, minus)) if kind == "A" else ((1, minus), (-1, plus)):
            chains.append((local, sign, length, first, kind + ("+" if sign > 0 else "-")))
            first += length
    order = [
        ring // 2 - (k + 1) // 2 if k % 2 == 1 else k // 2 + ring // 2 for k in range(ring)
    ]

    def z_copy(chain, step):
        _, sign, length, first, _ = chain
        return pltpu.make_async_remote_copy(
            src_ref=z_in.at[first + step - 1] if step else z_out.at[chains.index(chain)],
            dst_ref=z_in.at[first + step],
            send_sem=z_send_sem.at[first + step],
            recv_sem=z_recv_sem.at[first + step],
            device_id={"dp": up if sign > 0 else down},
            device_id_type=MESH,
        )

    def ready(chain, hop):
        _, sign, length, _, _ = chain
        return [offset % ring for offset in order].index(sign * (length - hop) % ring)

    def own_part(local, step):
        return acc[step % ACC_SLOTS, local].reshape(groups, GROUP, width)

    def z_received(chain, step):
        z_copy(chain, step).wait_recv()
        place = chain[3] + step
        codes = z_in[place, pl.ds(0, passage_len)].astype(jnp.int32).astype(jnp.float32)
        scale_code = z_in[place, pl.ds(passage_len, CODE_ROWS)].astype(jnp.int32)
        scale = scale_of(scale_code.astype(jnp.float32)[:groups])
        return codes.reshape(groups, GROUP, width) * scale[:, None, :]

    def z_hop(chain, step):
        part = own_part(chain[0], ready(chain, step))
        if step:
            part = part + z_received(chain, step - 1)
        codes, scale_code = to_codes(part)
        message = z_in.at[chain[3] + step - 1] if step else z_out.at[chains.index(chain)]
        message[pl.ds(0, passage_len)] = codes.reshape(passage_len, width)
        if groups < CODE_ROWS:
            scale_code = jnp.concatenate(
                [scale_code, jnp.zeros((CODE_ROWS - groups, width), jnp.float32)], 0
            )
        message[pl.ds(passage_len, CODE_ROWS)] = scale_code.astype(jnp.int32).astype(
            jnp.int16
        )
        z_copy(chain, step).start()

    def code_pieces(slot):
        codes, scale_code = to_codes(grad_t[...].T.reshape(rows, tokens, width))
        group, inner = slot // group_slots, slot % group_slots
        for tile in range(tiles):
            back_out[group, :, inner * tiles + tile] = codes[
                :, tile * CODE_ROWS : (tile + 1) * CODE_ROWS
            ]
        back_scales[slot] = scale_code

    def early_gradient(slot, _):
        for start in range(0, flat, chunk):
            here = pl.ds(start, chunk)
            grad_t[:, here] = sum(
                products[slot, c, :, here] * totals[slot, c : c + 1, here]
                for c in range(per_block)
            )
        code_pieces(slot)
        return 0

    def late_gradient(slot, _):
        block = my_block(slot)
        for start in range(0, flat, chunk):
            here = pl.ds(start, chunk)
            grad_t[:, here] = sum(
                product(slot, block, c, here) * totals[slot, c : c + 1, here]
                for c in range(per_block)
            )
        code_pieces(slot)
        return 0

    def start_back(group):
        filler = jnp.zeros((rows, width), jnp.float32)
        stacked = jnp.stack(
            [
                back_scales[group * group_slots + k] if k < group_slots else filler
                for k in range(CODE_ROWS)
            ],
            1,
        )
        back_out[group, :, group_slots * tiles] = stacked.astype(jnp.int32).astype(jnp.int16)

        def send_back(offset, _):
            peer = peer_of(offset)
            pltpu.make_async_remote_copy(
                src_ref=back_out.at[group, peer],
                dst_ref=back_in.at[group, me],
                send_sem=send_sem.at[2 + group],
                recv_sem=back_sem.at[group],
                device_id={"cand": peer},
                device_id_type=MESH,
            ).start()
            return 0

        lax.fori_loop(1, rows, send_back, 0)
        back_in[group, me] = back_out[group, me]

    def passage_at(step):
        near = jnp.where(step % 2 == 1, ring // 2 - (step + 1) // 2, step // 2 + ring // 2)
        return lax.rem(plane + near, ring)

    def prepare(buffer, slot, c):
        value = q_turned[slot].astype(jnp.float32) * totals[slot, pl.ds(c, 1)]
        value_high = value.astype(jnp.bfloat16)
        buffer[:width] = value_high
        buffer[width:] = (value - value_high.astype(jnp.float32)).astype(jnp.bfloat16)

    prepare(scaled_even, 0, passage_at(0))

    def gradients(step, _):
        c = passage_at(step)
        sums = [0.0] * blocks_here
        for slot in range(cap):
            now, later = (
                (scaled_even, scaled_odd) if slot % 2 == 0 else (scaled_odd, scaled_even)
            )
            if slot < cap - 1:
                prepare(later, slot + 1, c)
            else:
                prepare(later, 0, passage_at(lax.rem(step + 1, per_block)))
            along = (((1,), (1,)), ((), ()))
            first = lax.dot_general(
                high[slot, c], now[...], along, preferred_element_type=jnp.float32
            )
            second = lax.dot_general(
                low[slot, c], now[:width], along, preferred_element_type=jnp.float32
            )
            passage_grad = first[:, :width] + first[:, width:] + second
            for local in range(blocks_here):
                chosen = jnp.where(my_block(slot) == local, 1.0, 0.0)
                sums[local] = sums[local] + chosen * passage_grad
        for local in range(blocks_here):
            acc[step % ACC_SLOTS, local] = sums[local]

        for k, actions in enumerate(SCHEDULES[ring]):
            if actions:

                @pl.when(step == k)
                def _(actions=actions):
                    for action in actions:
                        act(action)

        return 0

    def act(action):
        kind, number = action[:-1], int(action[-1])
        if kind == "e":
            early_gradient(number, 0)
        elif kind == "l":
            late_gradient(number, 0)
        elif kind == "k":
            start_back(number)
        else:
            for chain in chains:
                if chain[4] == kind:
                    z_hop(chain, number)

    lax.fori_loop(0, per_block, gradients, 0)

    lane_at = lax.broadcasted_iota(jnp.int32, (per_block, LANES), 1)
    request_lane = lax.broadcasted_iota(jnp.int32, (per_block, 2 * row_blocks), 1)
    logits = jnp.zeros((per_block, 2 * row_blocks), jnp.float32)
    for request in range(2 * row_blocks):
        place = place_of(request)
        mine = lane_at == (place % cap) * rows + me
        value = jnp.sum(jnp.where(mine, scores[place // cap], 0.0), 1, keepdims=True)
        logits = jnp.where(request_lane == request, value, logits)
    first, second = logits[:, :row_blocks], logits[:, row_blocks:]
    log_total = jnp.log(
        jnp.sum(jnp.exp(first), 0, keepdims=True) + jnp.sum(jnp.exp(second), 0, keepdims=True)
    )
    square = (row_blocks, row_blocks)
    diagonal = lax.broadcasted_iota(jnp.int32, square, 0) == lax.broadcasted_iota(
        jnp.int32, square, 1
    )
    my_column = lax.broadcasted_iota(jnp.int32, pos_ref.shape, 1) == me
    positive = jnp.sum(jnp.where(my_column, pos_ref[...], 0), 1, keepdims=True)
    positive = jnp.sum(jnp.where(diagonal, positive, 0), 0, keepdims=True)
    candidate = lax.broadcasted_iota(jnp.int32, (per_block, row_blocks), 0)
    chosen = jnp.where(candidate == positive, first, 0.0) + jnp.where(
        candidate + per_block == positive, second, 0.0
    )
    loss_ref[...] = log_total - jnp.sum(chosen, 0, keepdims=True)

    for local in range(blocks_here):
        result = own_part(local, per_block - 1)
        for chain in chains:
            if chain[0] == local and chain[2]:
                result = result + z_received(chain, chain[2] - 1)
        passage_out[local] = result.reshape(passage_len, width)

    for group in range(2):
        back_others = back_in.at[group, others]
        pltpu.make_async_copy(back_others, back_others, back_sem.at[group]).wait()
    scale_row = lax.broadcasted_iota(jnp.int32, (CODE_ROWS, width), 0)

    def piece(place):
        owner, slot = place // cap, place % cap
        group, inner = slot // group_slots, slot % group_slots
        codes = [back_in[group, owner, inner * tiles + tile] for tile in range(tiles)]
        codes = jnp.concatenate([c.astype(jnp.int32) for c in codes], 0).astype(jnp.float32)
        scale_code = back_in[group, owner, group_slots * tiles].astype(jnp.int32)
        scale_code = jnp.sum(jnp.where(scale_row == inner, scale_code, 0), 0, keepdims=True)
        return codes * scale_of(scale_code.astype(jnp.float32))

    def add_pair(block_row, _):
        second = place_of(row_blocks + block_row)
        query_out[block_row] = piece(place_of(block_row)) + piece(second)
        return 0

    lax.fori_loop(0, row_blocks, add_pair, 0)

    for group in range(cap // q_group):
        q_wait(group, send_sem.at[0])
    pltpu.make_async_copy(scores.at[others], scores.at[others], send_sem.at[1]).wait()
    for group in range(2):
        back_others = back_in.at[group, others]
        pltpu.make_async_copy(back_others, back_others, send_sem.at[2 + group]).wait()
    for chain in chains:
        for step in range(chain[2]):
            z_copy(chain, step).wait_send()


def finish_kernel(*refs):
    for source, target in zip(refs[:3], refs[3:]):
        target[...] = source[...]


def on_device(rows, ring, queries, passages, cand_ids, pos_index):
    row_blocks, _, tokens, width = queries.shape
    blocks_here, per_block, passage_len, _ = passages.shape
    requests = 2 * row_blocks
    cap = 4 * ((requests + rows - 1) // rows)
    flat = rows * tokens
    vmem = pl.BlockSpec(memory_space=pltpu.VMEM)
    hops = blocks_here * (ring - 1)
    f32, bf16, i16 = jnp.float32, jnp.bfloat16, jnp.int16
    out_shape = (
        jax.ShapeDtypeStruct((1, row_blocks), f32),
        jax.ShapeDtypeStruct((row_blocks, tokens, width), f32),
        jax.ShapeDtypeStruct((blocks_here, passage_len, width), f32),
    )
    z_rows = passage_len + CODE_ROWS
    back_tiles = cap // 2 * tokens // CODE_ROWS + 1
    results = pl.pallas_call(
        functools.partial(main_kernel, rows, ring, cap),
        out_shape=out_shape,
        in_specs=[vmem] * 4,
        out_specs=(vmem, vmem, vmem),
        scratch_shapes=[
            pltpu.VMEM((8, LANES), jnp.int32),
            pltpu.SMEM((8, LANES), jnp.int32),
            pltpu.VMEM((cap // Q_GROUP, rows, Q_GROUP, tokens, width), bf16),
            pltpu.VMEM((cap, flat, width), bf16),
            pltpu.VMEM((cap, width, flat), bf16),
            pltpu.VMEM((blocks_here, per_block, width, passage_len), bf16),
            pltpu.VMEM((cap, per_block, passage_len, flat), bf16),
            pltpu.VMEM((cap, per_block, passage_len, flat), bf16),
            pltpu.VMEM((cap, per_block, flat), f32),
            pltpu.VMEM((rows, per_block, LANES), f32),
            pltpu.VMEM((cap // 2 + 1, per_block, width, flat), f32),
            pltpu.VMEM((2 * width, flat), bf16),
            pltpu.VMEM((2 * width, flat), bf16),
            pltpu.VMEM((width, flat), f32),
            pltpu.VMEM((cap, rows, width), f32),
            pltpu.VMEM((2, rows, back_tiles, CODE_ROWS, width), i16),
            pltpu.VMEM((2, rows, back_tiles, CODE_ROWS, width), i16),
            pltpu.VMEM((ACC_SLOTS, blocks_here, passage_len, width), f32),
            pltpu.VMEM((2 * blocks_here, z_rows, width), i16),
            pltpu.VMEM((hops, z_rows, width), i16),
            pltpu.SemaphoreType.DMA,
            pltpu.SemaphoreType.DMA((4,)),
            pltpu.SemaphoreType.DMA((cap // Q_GROUP,)),
            pltpu.SemaphoreType.DMA,
            pltpu.SemaphoreType.DMA((2,)),
            pltpu.SemaphoreType.DMA((hops,)),
            pltpu.SemaphoreType.DMA((hops,)),
        ],
        compiler_params=pltpu.CompilerParams(
            collective_id=0, has_side_effects=True, vmem_limit_bytes=63 * 1024 * 1024
        ),
        name="late_interaction",
    )(
        cand_ids.T,
        queries.reshape(row_blocks, tokens, width),
        passages,
        pos_index,
    )
    losses, query_grads, passage_grads = pl.pallas_call(
        finish_kernel,
        out_shape=out_shape,
        in_specs=[vmem] * 3,
        out_specs=(vmem, vmem, vmem),
        name="results",
    )(*results)
    return (losses.reshape(row_blocks, 1), query_grads[:, None], passage_grads[:, None])


def solution(mesh):
    in_specs = (
        P("dp", "cand", None, None),
        P("cand", None, None, None),
        P("dp", None),
        P("dp", None),
    )
    out_specs = (P("dp", "cand"), P("dp", "cand", None, None), P("cand", "dp", None, None))
    return jax.shard_map(
        functools.partial(on_device, mesh.shape["cand"], mesh.shape["dp"]),
        mesh=mesh,
        in_specs=in_specs,
        out_specs=out_specs,
        check_vma=False,
    )
```

```python
import functools
import math

import jax
import jax.numpy as jnp
from jax import lax
from jax.experimental import pallas as pl
from jax.experimental.pallas import tpu as pltpu
from jax.sharding import PartitionSpec as P

softness = 0.05
loss_scale = 32.0
to_exp2 = math.log2(math.e) / softness
MESH = pl.DeviceIdType.MESH
HIGHEST = lax.Precision.HIGHEST
LANES = 128
CODE_ROWS = 16
SCALE_STEPS = 256.0
TOP = 32700.0
TINY = 1e-30
GROUP = 32
CHUNK = 256
Q_GROUP = 1
ACC_SLOTS = 3
SCHEDULES = {
    8: (
        ("A+0", "B-0"),
        ("B+0", "e0"),
        ("A-0", "e1", "k0", "A+1", "B-1"),
        ("e2",),
        ("B+1", "A-1"),
        ("l3", "k1", "A+2", "B-2"),
        ("B+2", "A-2", "A+3", "B-3"),
        (),
    ),
    4: (
        ("A+0", "B-0"),
        ("B+0", "e0", "e1", "k0"),
        ("A-0", "A+1", "B-1", "l2"),
        ("l3", "k1"),
    ),
}


def to_codes(values):
    top = jnp.maximum(jnp.max(jnp.abs(values), 1), TINY)
    scale_code = jnp.ceil(SCALE_STEPS * (jnp.log2(top) - math.log2(TOP)))
    inverse = jnp.exp2(scale_code * (-1.0 / SCALE_STEPS))
    codes = jnp.round(values * inverse[:, None, :]).astype(jnp.int32).astype(jnp.int16)
    return codes, scale_code


def scale_of(scale_code):
    return jnp.exp2(scale_code * (1.0 / SCALE_STEPS))


def fill_tables(blocks_here, cap, ids_ref, table):
    count = ids_ref.shape[0] * ids_ref.shape[1]
    along = lax.broadcasted_iota(jnp.int32, (count, LANES), 1)
    down = lax.broadcasted_iota(jnp.int32, (count, LANES), 0)
    row_blocks = ids_ref.shape[1]
    halves = [jnp.broadcast_to(ids_ref[h : h + 1], (row_blocks, row_blocks)) for h in range(2)]
    square = (row_blocks, row_blocks)
    diagonal = lax.broadcasted_iota(jnp.int32, square, 0) == lax.broadcasted_iota(
        jnp.int32, square, 1
    )
    columns = [jnp.sum(jnp.where(diagonal, half, 0), 1, keepdims=True) for half in halves]
    ids_down = jnp.broadcast_to(jnp.concatenate(columns, 0), (count, LANES))
    owner_down = ids_down // blocks_here
    owner_along = jnp.sum(jnp.where(along == down, owner_down, 0), 0, keepdims=True)
    same = (owner_along == owner_down) & (along < count)
    rank_along = jnp.sum((same & (down < along)).astype(jnp.int32), 0, keepdims=True)
    place_along = owner_along * cap + rank_along
    rank_down = jnp.sum((same & (along < down)).astype(jnp.int32), 1, keepdims=True)
    here = owner_down * cap + rank_down == along
    request_along = jnp.sum(jnp.where(here, down + 1, 0), 0, keepdims=True) - 1
    block_along = jnp.sum(jnp.where(here, ids_down % blocks_here, 0), 0, keepdims=True)
    row = lax.broadcasted_iota(jnp.int32, table.shape, 0)
    table[...] = jnp.where(
        row == 0, request_along, jnp.where(row == 1, place_along, block_along)
    )


def main_kernel(
    rows,
    ring,
    cap,
    ids_ref,
    q_ref,
    p_ref,
    pos_ref,
    loss_ref,
    query_out,
    passage_out,
    table,
    table_s,
    q_send,
    q_slot,
    q_turned,
    p_turned,
    high,
    low,
    totals,
    scores,
    products,
    scaled_even,
    scaled_odd,
    grad_t,
    back_scales,
    back_out,
    back_in,
    acc,
    z_out,
    z_in,
    table_sem,
    send_sem,
    q_sem,
    score_sem,
    back_sem,
    z_send_sem,
    z_recv_sem,
):
    row_blocks, tokens, width = q_ref.shape
    blocks_here, per_block, passage_len, _ = p_ref.shape
    flat = rows * tokens
    chunk = min(CHUNK, flat)
    me = lax.axis_index("cand")
    plane = lax.axis_index("dp")
    groups = passage_len // GROUP
    tiles = tokens // CODE_ROWS
    group_slots = cap // 2

    head = pl.ds(0, flat - tokens)
    q_group = q_send.shape[2]

    def peer_of(offset):
        return lax.rem(me + offset, rows)

    barrier = pltpu.get_barrier_semaphore()

    def greet(offset, _):
        pl.semaphore_signal(
            barrier, inc=1, device_id={"cand": peer_of(offset)}, device_id_type=MESH
        )
        return 0

    lax.fori_loop(1, rows, greet, 0)
    up, down = lax.rem(plane + 1, ring), lax.rem(plane + ring - 1, ring)
    for neighbour in (up, down):
        pl.semaphore_signal(barrier, inc=1, device_id={"dp": neighbour}, device_id_type=MESH)

    fill_tables(blocks_here, cap, ids_ref, table)
    to_scalars = pltpu.make_async_copy(table, table_s, table_sem)
    to_scalars.start()
    to_scalars.wait()

    def request_at(place):
        return table_s[0, place]

    def place_of(request):
        return table_s[1, request]

    def fill(owner, _):
        for slot in range(cap):
            request = jnp.maximum(request_at(owner * cap + slot), 0)
            q_send[slot // q_group, owner, slot % q_group] = q_ref[request % row_blocks]
        return 0

    lax.fori_loop(0, rows, fill, 0)
    my_rows = pl.ds(pl.multiple_of(me * tokens, tokens), tokens)
    pl.semaphore_wait(barrier, rows - 1 + 2)

    def send_group(group):
        slots = pl.ds(group * q_group, q_group)

        def send_queries(offset, _):
            peer = peer_of(offset)
            pltpu.make_async_remote_copy(
                src_ref=q_send.at[group, peer],
                dst_ref=q_slot.at[slots, my_rows],
                send_sem=send_sem.at[0],
                recv_sem=q_sem.at[group],
                device_id={"cand": peer},
                device_id_type=MESH,
            ).start()
            return 0

        lax.fori_loop(1, rows, send_queries, 0)

    def q_wait(group, sem):
        arrived = q_slot.at[pl.ds(group * q_group, q_group), head]
        pltpu.make_async_copy(arrived, arrived, sem).wait()

    for group in range(cap // q_group):
        send_group(group)
    for slot in range(cap):
        q_slot[slot, my_rows] = q_send[slot // q_group, me, slot % q_group]

    def turn_passage(c, _):
        for block in range(blocks_here):
            p_turned[block, c] = p_ref[block, c].T
        return 0

    lax.fori_loop(0, per_block, turn_passage, 0)

    lane = lax.broadcasted_iota(jnp.int32, (flat, LANES), 1)
    query_of = lax.broadcasted_iota(jnp.int32, (flat, LANES), 0) // tokens
    my_scores = jnp.zeros((per_block, LANES), jnp.float32)

    def my_request(slot):
        return request_at(me * cap + slot)

    def my_block(slot):
        return table_s[2, me * cap + slot]

    early = products.shape[0]

    def product(slot, block, c, here):
        passage = p_turned[block, c]
        return jnp.dot(
            passage, high[slot, c, :, here], preferred_element_type=jnp.float32
        ) + jnp.dot(passage, low[slot, c, :, here], preferred_element_type=jnp.float32)

    def early_products(slot, _):
        block = my_block(slot)
        for c in range(per_block):
            for start in range(0, flat, chunk):
                here = pl.ds(start, chunk)
                products[slot, c, :, here] = product(slot, block, c, here)
        return 0

    def forward(slot, my_scores):
        @pl.when(lax.rem(slot, q_group) == 0)
        def _():
            q_wait(slot // q_group, q_sem.at[slot // q_group])

        block = my_block(slot)
        q_turned[slot] = q_slot[slot].T

        for c in range(per_block):
            passage = p_ref[block, c]
            for start in range(0, flat, chunk):
                here = pl.ds(start, chunk)
                similar = jnp.dot(
                    passage, q_turned[slot, :, here], preferred_element_type=jnp.float32
                )
                exponent = jnp.exp2(similar * to_exp2)
                rounded = exponent.astype(jnp.bfloat16)
                high[slot, c, :, here] = rounded
                low[slot, c, :, here] = (exponent - rounded.astype(jnp.float32)).astype(
                    jnp.bfloat16
                )
                totals[slot, c : c + 1, here] = jnp.sum(exponent, 0, keepdims=True)
        soft_max = softness * jnp.log(totals[slot])
        @pl.when(slot == 0)
        def _():
            early_products(0, 0)

        place = (query_of + slot * rows == lane).astype(jnp.float32)
        return my_scores + jnp.dot(
            soft_max, place, precision=HIGHEST, preferred_element_type=jnp.float32
        )

    my_scores = lax.fori_loop(0, cap, forward, my_scores)
    scores[me] = my_scores

    def send_scores(offset, _):
        pltpu.make_async_remote_copy(
            src_ref=scores.at[me],
            dst_ref=scores.at[me],
            send_sem=send_sem.at[1],
            recv_sem=score_sem,
            device_id={"cand": peer_of(offset)},
            device_id_type=MESH,
        ).start()
        return 0

    lax.fori_loop(1, rows, send_scores, 0)
    lax.fori_loop(1, early, early_products, 0)
    others = pl.ds(0, rows - 1)
    pltpu.make_async_copy(scores.at[others], scores.at[others], score_sem).wait()

    lane_in = lax.broadcasted_iota(jnp.int32, (LANES, rows), 0)
    query_in = lax.broadcasted_iota(jnp.int32, (LANES, rows), 1)

    def scores_of(place):
        pick = (lane_in == query_in + (place % cap) * rows).astype(jnp.float32)
        return jnp.dot(
            scores[place // cap], pick, precision=HIGHEST, preferred_element_type=jnp.float32
        )

    column = lax.broadcasted_iota(jnp.int32, (per_block, rows), 0)
    spread = (
        lax.broadcasted_iota(jnp.int32, (rows, flat), 1) // tokens
        == lax.broadcasted_iota(jnp.int32, (rows, flat), 0)
    ).astype(jnp.float32)

    position_row = lax.broadcasted_iota(jnp.int32, pos_ref.shape, 0)

    def positives(block_row):
        return jnp.sum(jnp.where(position_row == block_row, pos_ref[...], 0), 0, keepdims=True)

    def factors(slot, _):
        request = my_request(slot)
        valid = jnp.where(request >= 0, loss_scale, 0.0)
        request = jnp.maximum(request, 0)
        block_row, half = request % row_blocks, request // row_blocks
        mine = scores_of(me * cap + slot)
        other = scores_of(place_of((1 - half) * row_blocks + block_row))
        log_total = jnp.log(
            jnp.sum(jnp.exp(mine), 0, keepdims=True) + jnp.sum(jnp.exp(other), 0, keepdims=True)
        )
        onehot = (column + half * per_block == positives(block_row)).astype(jnp.float32)
        dlogit = valid * (jnp.exp(mine - log_total) - onehot)
        wide = jnp.dot(dlogit, spread, precision=HIGHEST, preferred_element_type=jnp.float32)
        totals[slot] = wide / totals[slot]
        return 0

    lax.fori_loop(0, cap, factors, 0, unroll=True)

    plus, minus = ring // 2, ring - 1 - ring // 2
    chains = []
    first = 0
    for local in range(blocks_here):
        kind = "A" if local < blocks_here // 2 else "B"
        for sign, length in ((1, plus), (-1, minus)) if kind == "A" else ((1, minus), (-1, plus)):
            chains.append((local, sign, length, first, kind + ("+" if sign > 0 else "-")))
            first += length
    order = [
        ring // 2 - (k + 1) // 2 if k % 2 == 1 else k // 2 + ring // 2 for k in range(ring)
    ]

    def z_copy(chain, step):
        _, sign, length, first, _ = chain
        return pltpu.make_async_remote_copy(
            src_ref=z_in.at[first + step - 1] if step else z_out.at[chains.index(chain)],
            dst_ref=z_in.at[first + step],
            send_sem=z_send_sem.at[first + step],
            recv_sem=z_recv_sem.at[first + step],
            device_id={"dp": up if sign > 0 else down},
            device_id_type=MESH,
        )

    def ready(chain, hop):
        _, sign, length, _, _ = chain
        return [offset % ring for offset in order].index(sign * (length - hop) % ring)

    def own_part(local, step):
        return acc[step % ACC_SLOTS, local].reshape(groups, GROUP, width)

    def z_received(chain, step):
        z_copy(chain, step).wait_recv()
        place = chain[3] + step
        codes = z_in[place, pl.ds(0, passage_len)].astype(jnp.int32).astype(jnp.float32)
        scale_code = z_in[place, pl.ds(passage_len, CODE_ROWS)].astype(jnp.int32)
        scale = scale_of(scale_code.astype(jnp.float32)[:groups])
        return codes.reshape(groups, GROUP, width) * scale[:, None, :]

    def z_hop(chain, step):
        part = own_part(chain[0], ready(chain, step))
        if step:
            part = part + z_received(chain, step - 1)
        codes, scale_code = to_codes(part)
        message = z_in.at[chain[3] + step - 1] if step else z_out.at[chains.index(chain)]
        message[pl.ds(0, passage_len)] = codes.reshape(passage_len, width)
        if groups < CODE_ROWS:
            scale_code = jnp.concatenate(
                [scale_code, jnp.zeros((CODE_ROWS - groups, width), jnp.float32)], 0
            )
        message[pl.ds(passage_len, CODE_ROWS)] = scale_code.astype(jnp.int32).astype(
            jnp.int16
        )
        z_copy(chain, step).start()

    def code_pieces(slot):
        codes, scale_code = to_codes(grad_t[...].T.reshape(rows, tokens, width))
        group, inner = slot // group_slots, slot % group_slots
        for tile in range(tiles):
            back_out[group, :, inner * tiles + tile] = codes[
                :, tile * CODE_ROWS : (tile + 1) * CODE_ROWS
            ]
        back_scales[slot] = scale_code

    def early_gradient(slot, _):
        for start in range(0, flat, chunk):
            here = pl.ds(start, chunk)
            grad_t[:, here] = sum(
                products[slot, c, :, here] * totals[slot, c : c + 1, here]
                for c in range(per_block)
            )
        code_pieces(slot)
        return 0

    def late_gradient(slot, _):
        block = my_block(slot)
        for start in range(0, flat, chunk):
            here = pl.ds(start, chunk)
            grad_t[:, here] = sum(
                product(slot, block, c, here) * totals[slot, c : c + 1, here]
                for c in range(per_block)
            )
        code_pieces(slot)
        return 0

    def start_back(group):
        filler = jnp.zeros((rows, width), jnp.float32)
        stacked = jnp.stack(
            [
                back_scales[group * group_slots + k] if k < group_slots else filler
                for k in range(CODE_ROWS)
            ],
            1,
        )
        back_out[group, :, group_slots * tiles] = stacked.astype(jnp.int32).astype(jnp.int16)

        def send_back(offset, _):
            peer = peer_of(offset)
            pltpu.make_async_remote_copy(
                src_ref=back_out.at[group, peer],
                dst_ref=back_in.at[group, me],
                send_sem=send_sem.at[2 + group],
                recv_sem=back_sem.at[group],
                device_id={"cand": peer},
                device_id_type=MESH,
            ).start()
            return 0

        lax.fori_loop(1, rows, send_back, 0)
        back_in[group, me] = back_out[group, me]

    def passage_at(step):
        near = jnp.where(step % 2 == 1, ring // 2 - (step + 1) // 2, step // 2 + ring // 2)
        return lax.rem(plane + near, ring)

    def prepare(buffer, slot, c):
        value = q_turned[slot].astype(jnp.float32) * totals[slot, pl.ds(c, 1)]
        value_high = value.astype(jnp.bfloat16)
        buffer[:width] = value_high
        buffer[width:] = (value - value_high.astype(jnp.float32)).astype(jnp.bfloat16)

    prepare(scaled_even, 0, passage_at(0))

    def gradients(step, _):
        c = passage_at(step)
        sums = [0.0] * blocks_here
        for slot in range(cap):
            now, later = (
                (scaled_even, scaled_odd) if slot % 2 == 0 else (scaled_odd, scaled_even)
            )
            if slot < cap - 1:
                prepare(later, slot + 1, c)
            else:
                prepare(later, 0, passage_at(lax.rem(step + 1, per_block)))
            along = (((1,), (1,)), ((), ()))
            first = lax.dot_general(
                high[slot, c], now[...], along, preferred_element_type=jnp.float32
            )
            second = lax.dot_general(
                low[slot, c], now[:width], along, preferred_element_type=jnp.float32
            )
            passage_grad = first[:, :width] + first[:, width:] + second
            for local in range(blocks_here):
                chosen = jnp.where(my_block(slot) == local, 1.0, 0.0)
                sums[local] = sums[local] + chosen * passage_grad
        for local in range(blocks_here):
            acc[step % ACC_SLOTS, local] = sums[local]

        for k, actions in enumerate(SCHEDULES[ring]):
            if actions:

                @pl.when(step == k)
                def _(actions=actions):
                    for action in actions:
                        act(action)

        return 0

    def act(action):
        kind, number = action[:-1], int(action[-1])
        if kind == "e":
            early_gradient(number, 0)
        elif kind == "l":
            late_gradient(number, 0)
        elif kind == "k":
            start_back(number)
        else:
            for chain in chains:
                if chain[4] == kind:
                    z_hop(chain, number)

    lax.fori_loop(0, per_block, gradients, 0)

    lane_at = lax.broadcasted_iota(jnp.int32, (per_block, LANES), 1)
    request_lane = lax.broadcasted_iota(jnp.int32, (per_block, 2 * row_blocks), 1)
    logits = jnp.zeros((per_block, 2 * row_blocks), jnp.float32)
    for request in range(2 * row_blocks):
        place = place_of(request)
        mine = lane_at == (place % cap) * rows + me
        value = jnp.sum(jnp.where(mine, scores[place // cap], 0.0), 1, keepdims=True)
        logits = jnp.where(request_lane == request, value, logits)
    first, second = logits[:, :row_blocks], logits[:, row_blocks:]
    log_total = jnp.log(
        jnp.sum(jnp.exp(first), 0, keepdims=True) + jnp.sum(jnp.exp(second), 0, keepdims=True)
    )
    square = (row_blocks, row_blocks)
    diagonal = lax.broadcasted_iota(jnp.int32, square, 0) == lax.broadcasted_iota(
        jnp.int32, square, 1
    )
    my_column = lax.broadcasted_iota(jnp.int32, pos_ref.shape, 1) == me
    positive = jnp.sum(jnp.where(my_column, pos_ref[...], 0), 1, keepdims=True)
    positive = jnp.sum(jnp.where(diagonal, positive, 0), 0, keepdims=True)
    candidate = lax.broadcasted_iota(jnp.int32, (per_block, row_blocks), 0)
    chosen = jnp.where(candidate == positive, first, 0.0) + jnp.where(
        candidate + per_block == positive, second, 0.0
    )
    loss_ref[...] = log_total - jnp.sum(chosen, 0, keepdims=True)

    for group in range(2):
        back_others = back_in.at[group, others]
        pltpu.make_async_copy(back_others, back_others, back_sem.at[group]).wait()
    scale_row = lax.broadcasted_iota(jnp.int32, (CODE_ROWS, width), 0)

    def piece(place):
        owner, slot = place // cap, place % cap
        group, inner = slot // group_slots, slot % group_slots
        codes = [back_in[group, owner, inner * tiles + tile] for tile in range(tiles)]
        codes = jnp.concatenate([c.astype(jnp.int32) for c in codes], 0).astype(jnp.float32)
        scale_code = back_in[group, owner, group_slots * tiles].astype(jnp.int32)
        scale_code = jnp.sum(jnp.where(scale_row == inner, scale_code, 0), 0, keepdims=True)
        return codes * scale_of(scale_code.astype(jnp.float32))

    def add_pair(block_row, _):
        second = place_of(row_blocks + block_row)
        query_out[block_row] = piece(place_of(block_row)) + piece(second)
        return 0

    lax.fori_loop(0, row_blocks, add_pair, 0, unroll=4)

    for local in range(blocks_here):
        result = own_part(local, per_block - 1)
        for chain in chains:
            if chain[0] == local and chain[2]:
                result = result + z_received(chain, chain[2] - 1)
        passage_out[local] = result.reshape(passage_len, width)

    for group in range(cap // q_group):
        q_wait(group, send_sem.at[0])
    pltpu.make_async_copy(scores.at[others], scores.at[others], send_sem.at[1]).wait()
    for group in range(2):
        back_others = back_in.at[group, others]
        pltpu.make_async_copy(back_others, back_others, send_sem.at[2 + group]).wait()
    for chain in chains:
        for step in range(chain[2]):
            z_copy(chain, step).wait_send()


def finish_kernel(*refs):
    for source, target in zip(refs[:3], refs[3:]):
        target[...] = source[...]


def on_device(rows, ring, queries, passages, cand_ids, pos_index):
    row_blocks, _, tokens, width = queries.shape
    blocks_here, per_block, passage_len, _ = passages.shape
    requests = 2 * row_blocks
    cap = 4 * ((requests + rows - 1) // rows)
    flat = rows * tokens
    vmem = pl.BlockSpec(memory_space=pltpu.VMEM)
    hops = blocks_here * (ring - 1)
    f32, bf16, i16 = jnp.float32, jnp.bfloat16, jnp.int16
    out_shape = (
        jax.ShapeDtypeStruct((1, row_blocks), f32),
        jax.ShapeDtypeStruct((row_blocks, tokens, width), f32),
        jax.ShapeDtypeStruct((blocks_here, passage_len, width), f32),
    )
    z_rows = passage_len + CODE_ROWS
    back_tiles = cap // 2 * tokens // CODE_ROWS + 1
    results = pl.pallas_call(
        functools.partial(main_kernel, rows, ring, cap),
        out_shape=out_shape,
        in_specs=[vmem] * 4,
        out_specs=(vmem, vmem, vmem),
        scratch_shapes=[
            pltpu.VMEM((8, LANES), jnp.int32),
            pltpu.SMEM((8, LANES), jnp.int32),
            pltpu.VMEM((cap // Q_GROUP, rows, Q_GROUP, tokens, width), bf16),
            pltpu.VMEM((cap, flat, width), bf16),
            pltpu.VMEM((cap, width, flat), bf16),
            pltpu.VMEM((blocks_here, per_block, width, passage_len), bf16),
            pltpu.VMEM((cap, per_block, passage_len, flat), bf16),
            pltpu.VMEM((cap, per_block, passage_len, flat), bf16),
            pltpu.VMEM((cap, per_block, flat), f32),
            pltpu.VMEM((rows, per_block, LANES), f32),
            pltpu.VMEM((cap // 2 + 1, per_block, width, flat), f32),
            pltpu.VMEM((2 * width, flat), bf16),
            pltpu.VMEM((2 * width, flat), bf16),
            pltpu.VMEM((width, flat), f32),
            pltpu.VMEM((cap, rows, width), f32),
            pltpu.VMEM((2, rows, back_tiles, CODE_ROWS, width), i16),
            pltpu.VMEM((2, rows, back_tiles, CODE_ROWS, width), i16),
            pltpu.VMEM((ACC_SLOTS, blocks_here, passage_len, width), f32),
            pltpu.VMEM((2 * blocks_here, z_rows, width), i16),
            pltpu.VMEM((hops, z_rows, width), i16),
            pltpu.SemaphoreType.DMA,
            pltpu.SemaphoreType.DMA((4,)),
            pltpu.SemaphoreType.DMA((cap // Q_GROUP,)),
            pltpu.SemaphoreType.DMA,
            pltpu.SemaphoreType.DMA((2,)),
            pltpu.SemaphoreType.DMA((hops,)),
            pltpu.SemaphoreType.DMA((hops,)),
        ],
        compiler_params=pltpu.CompilerParams(
            collective_id=0, has_side_effects=True, vmem_limit_bytes=63 * 1024 * 1024
        ),
        name="late_interaction",
    )(
        cand_ids.T,
        queries.reshape(row_blocks, tokens, width),
        passages,
        pos_index,
    )
    losses, query_grads, passage_grads = pl.pallas_call(
        finish_kernel,
        out_shape=out_shape,
        in_specs=[vmem] * 3,
        out_specs=(vmem, vmem, vmem),
        name="results",
    )(*results)
    return (losses.reshape(row_blocks, 1), query_grads[:, None], passage_grads[:, None])


def solution(mesh):
    in_specs = (
        P("dp", "cand", None, None),
        P("cand", None, None, None),
        P("dp", None),
        P("dp", None),
    )
    out_specs = (P("dp", "cand"), P("dp", "cand", None, None), P("cand", "dp", None, None))
    return jax.shard_map(
        functools.partial(on_device, mesh.shape["cand"], mesh.shape["dp"]),
        mesh=mesh,
        in_specs=in_specs,
        out_specs=out_specs,
        check_vma=False,
    )
```
